256 devices in a mesh: grp: 8 (over z), dev: 32 (over y, x, core).
Axes of the slice: x: 4, y: 4, z: 8, core: 2. Of those that a mesh axis runs over, the one named last changes fastest.
Arguments:
- encodings: bfloat16 [32768, 1024], P(('grp', 'dev')), may hold values from -6 to 6
- label_weights: bfloat16 [131072, 1024], P(('grp', 'dev')), may hold values from -0.1875 to 0.1875
- label_count: int32 [1024], P(('grp', 'dev')), may hold values from 32 to 128
- matched: int32 [32768, 8], P(('grp', 'dev')), may hold values from 0 to 1023, all different within a row; in each aligned block of 128 rows (0 to 127, 128 to 255, ...) at most 2 rows name the same one
- positive: int32 [32768, 8], P(('grp', 'dev')), may hold values from 0 to 127
Outputs:
- enc_grad: bfloat16 [32768, 1024], P(('grp', 'dev'))
- query_loss: float32 [32768], P(('grp', 'dev'))
- label_weight_gradient: float32 [131072, 1024], P(('grp', 'dev'))
The draws below stay inside these ranges and needn't reach their ends.
Inputs may be any that keep to these rules, and one draw needn't show every extreme that they name: The 8 ids of a query differ; among the 128 queries of one device no cluster is matched more than 2 times, and in every draw some cluster is matched exactly 2 times by one device's queries; every cluster is matched somewhere.
All inputs are finite; a program needn't handle non-finite values.
Results may differ from the reference program's by a relative error of at most 0.011.
Values may be sent and summed in bfloat16 or wider, within the bound.
No kernel may reach another device: no remote copies, remote signals or barrier semaphores. Data moves between devices by JAX's collectives and lax.ppermute only.
A program may use at most 64 MiB of HBM per device.

```python
import math
import jax
import jax.numpy as jnp
import numpy as np
from jax import lax

D = 1024
LB = 128
TOP = 8
Q_DEV = 128
CLUSTERS = 1024
TOKENS = 32768
MOST = 2


def place_ends(drawn, rng, least, top_value):
    place = [jax.random.randint(jax.random.fold_in(rng, axis), (), 0, length) for axis, length in enumerate(drawn.shape)]
    main_axis = drawn.shape.index(max(drawn.shape))
    next_to = place[:main_axis] + [(place[main_axis] + 1) % drawn.shape[main_axis]] + place[main_axis + 1:]
    return drawn.at[tuple(place)].set(least).at[tuple(next_to)].set(top_value)


def block_levels(rng, shape, split, smallest, top_value):
    factor_of = 1.0
    for dim, blocks in split:
        draws = jax.random.uniform(jax.random.fold_in(jax.random.fold_in(rng, 6), dim), (blocks,), jnp.float32, smallest / len(split), top_value / len(split))
        factor_of = factor_of * jnp.repeat(jnp.exp(draws), shape[dim] // blocks).reshape((-1,) + (1,) * (len(shape) - 1 - dim))
    return factor_of


def deal_out(own_key, own, number, rows, count, top, reach, slope):
    ranking = jax.random.permutation(own_key, count)
    crowded, ordinary = portions_of(count, rows * top, reach, slope, True), portions_of(count, rows * top, reach, slope, False)
    places = jnp.arange(count)

    def named(sizes, rotation):
        used = int((sizes > 0).sum())
        fixed = max(1, used // 4)
        shifted = fixed + (places - fixed + rotation * (used - fixed)) % max(1, count - fixed)
        return jnp.zeros((count,), jnp.int32).at[ranking[jnp.where(places < fixed, places, shifted)]].set(jnp.asarray(sizes, jnp.int32))

    sizes = jnp.where(number % 4 == 0, named(crowded, number // 4), named(ordinary, number - number // 4 - 1))
    mixed = jax.random.permutation(jax.random.fold_in(own, 3), count)
    giver, sink = mixed[0:count // 2 * 2:2], mixed[1:count // 2 * 2:2]
    margin = jnp.minimum(sizes[giver] - 1, reach - sizes[sink]) // 2
    margin = jnp.where((giver == ranking[0]) | (sink == ranking[0]) | (sizes[sink] == 0), 0, jnp.maximum(margin, 0))
    shifted = jax.random.randint(jax.random.fold_in(own, 4), (count // 2,), 0, 1 << 20) % (margin + 1)
    sizes = sizes.at[giver].add(-shifted).at[sink].add(shifted)
    items = jnp.searchsorted(jnp.cumsum(sizes), jnp.arange(rows * top), side="right").astype(jnp.int32)
    grid = items.reshape(top, rows).T
    grid = grid[jax.random.permutation(jax.random.fold_in(own, 1), rows)]
    rotation = jax.random.randint(jax.random.fold_in(own, 2), (rows, 1), 0, top)
    return jnp.take_along_axis(grid, (jnp.arange(top)[None, :] + rotation) % top, axis=1)


def portions_of(number_of, total, bound, skew, full):
    loads = [(1 << 20) // math.isqrt(rank ** skew) + 1 for rank in range(1, number_of + 1)]
    largest = bound if full else min(bound, max(-(-total // number_of), total * loads[0] // sum(loads)))
    least = 1 if total - largest >= number_of - 1 else 0
    holding, spare = [largest] + [least] * (number_of - 1), total - largest - least * (number_of - 1)
    while spare > 0:
        free = [i for i in range(1, number_of) if holding[i] < largest] or [i for i in range(1, number_of) if holding[i] < bound]
        pool, budget = sum([loads[i] for i in free]), spare
        for i in free:
            addition = min(bound - holding[i], max(1, budget * loads[i] // pool), spare)
            holding[i] = holding[i] + addition
            spare = spare - addition
    return np.array(holding)


def scatter_about(key, extent, width, limit, split=(), held_as=jnp.bfloat16):
    result = jax.random.normal(key, extent, jnp.float32) * width
    if len(split) > 0:
        result = block_levels(key, extent, split, -0.22, 0.18) * result
    return jnp.clip(result, min=-limit, max=limit).astype(held_as)


def setup_inputs(seed: int = 0) -> dict:
    streams_of = jax.random.split(jax.random.key(seed), 6)
    encodings = scatter_about(streams_of[0], (TOKENS, D), 1.0, 6.0, ((0, 256),))
    label_weights = scatter_about(streams_of[1], (CLUSTERS * LB, D), D ** -0.5, 0.1875, ((0, 256),))
    label_count = place_ends(jax.random.randint(streams_of[2], (CLUSTERS,), LB // 4, LB + 1), jax.random.fold_in(streams_of[2], 1), LB // 4, LB).astype(jnp.int32)
    matched_keys = jax.random.split(jax.random.fold_in(streams_of[3], 1), TOKENS // Q_DEV)
    matched_turns = jax.random.permutation(jax.random.fold_in(streams_of[3], 3), TOKENS // Q_DEV)
    matched = jax.vmap(lambda own, number: deal_out(jax.random.fold_in(streams_of[3], 2), own, number, Q_DEV, CLUSTERS, TOP, MOST, 2))(matched_keys, matched_turns).reshape((TOKENS, TOP))
    positive = place_ends(jax.random.randint(streams_of[4], (TOKENS, TOP), 0, LB), jax.random.fold_in(streams_of[4], 1), 0, LB - 1).astype(jnp.int32)
    return {"encodings": encodings, "label_weights": label_weights, "label_count": label_count, "matched": matched, "positive": positive}


def reference(encodings, label_weights, label_count, matched, positive):
    label_blocks = label_weights.reshape(CLUSTERS, LB, D)
    index = jnp.arange(LB, dtype=jnp.int32)
    block_rows = 32
    steps_count = TOKENS // block_rows

    def advance(weight_sum, pieces):
        enc, cluster_ids, wanted = pieces
        weights = label_blocks[cluster_ids].astype(jnp.float32)
        enc_wide = enc.astype(jnp.float32)
        label_scores = jnp.einsum('rd,rtld->rtl', enc_wide, weights)
        valid = index[None, None, :] < label_count[cluster_ids][:, :, None]
        target = (index[None, None, :] == wanted[:, :, None]).astype(jnp.float32)
        terms = jnp.where(valid, jax.nn.softplus(label_scores) - target * label_scores, jnp.float32(0.0))
        loss = jnp.sum(terms, axis=(1, 2)) / (TOP * LB)
        encoding_gradient = jnp.where(valid, jax.nn.sigmoid(label_scores) - target, jnp.float32(0.0)).astype(jnp.bfloat16)
        grad_wide = encoding_gradient.astype(jnp.float32)
        part_grad = jnp.einsum('rtl,rtld->rtd', grad_wide, weights).astype(jnp.bfloat16)
        enc_grad = jnp.sum(part_grad.astype(jnp.float32), axis=1).astype(jnp.bfloat16)
        wterm = jnp.einsum('rtl,rd->rtld', grad_wide, enc_wide)
        weight_sum = weight_sum.at[cluster_ids.reshape(-1)].add(wterm.reshape(-1, LB, D))
        return weight_sum, (enc_grad, loss)

    pieces = (encodings.reshape(steps_count, block_rows, D),
              matched.reshape(steps_count, block_rows, TOP),
              positive.reshape(steps_count, block_rows, TOP))
    start = jnp.zeros((CLUSTERS, LB, D), jnp.float32)
    weight_sum, step_outputs = lax.scan(advance, start, pieces)
    enc_grad = step_outputs[0].reshape(TOKENS, D)
    query_loss = step_outputs[1].reshape(TOKENS)
    return enc_grad, query_loss, weight_sum.reshape(CLUSTERS * LB, D)
```

```python
import functools

import jax
import jax.numpy as jnp
from jax import lax
from jax.experimental import pallas as pl
from jax.experimental.pallas import tpu as pltpu
from jax.sharding import PartitionSpec as P

F32 = jnp.float32
BF16 = jnp.bfloat16
EXTRA = 128
VMEM_LIMIT = 50 * 1024 * 1024


def iota(shape, dim):
    return lax.broadcasted_iota(jnp.int32, shape, dim)


def dispatch_kernel(grp_ref, x_ref, send_ref, pick_ref, *, top, per_dst):
    sources, queries, wide = x_ref.shape
    width = wide - EXTRA
    dsts = send_ref.shape[0]
    slots = 2 * per_dst
    rows = dsts * slots
    me = grp_ref[0].astype(F32)
    row = iota((rows, queries), 0)
    cluster = ((row // slots) * per_dst + row % per_dst).astype(F32)
    rank = ((row // per_dst) % 2).astype(F32)
    before = (iota((queries, queries), 0) < iota((queries, queries), 1)).astype(BF16)
    ones = jnp.ones((2 * queries, EXTRA), BF16)
    zero = jnp.zeros((dsts, slots, queries), F32)

    def one(source):
        meta = x_ref[source, :, width:].astype(F32).T
        group, local, slot = meta[0:top], meta[top : 2 * top], meta[2 * top : 3 * top]
        key = jnp.where(group == me, local, -1.0)
        want = slot + 1.0
        value = jnp.zeros((rows, queries), F32)
        for t in range(top):
            value = value + jnp.where(cluster == key[t : t + 1], want[t : t + 1], 0.0)
        hit = (value > 0.0).astype(BF16)
        earlier = jnp.dot(hit, before, preferred_element_type=F32)
        value = jnp.where(earlier == rank, value, 0.0)
        return value.reshape(dsts, slots, queries)

    for pair in range(sources // 2):
        a, b = one(2 * pair), one(2 * pair + 1)
        value = jnp.concatenate(
            [jnp.concatenate([a, zero], axis=2), jnp.concatenate([zero, b], axis=2)], axis=1
        ).reshape(2 * rows, 2 * queries)
        pick = (value > 0.0).astype(BF16)
        pick_ref[pair] = pick
        x = x_ref[2 * pair : 2 * pair + 2, :, 0:width].reshape(2 * queries, width)
        out = jnp.dot(pick, x, preferred_element_type=F32).astype(BF16)
        want = jnp.dot(value.astype(BF16), ones, preferred_element_type=F32).astype(BF16)
        at = pl.ds(pair * 2 * slots, 2 * slots)
        send_ref[:, at, 0:width] = out.reshape(dsts, 2 * slots, width)
        send_ref[:, at, width:] = want.reshape(dsts, 2 * slots, EXTRA)


def dispatch(x, grp, dsts, per_dst, top):
    sources, queries, wide = x.shape
    slots = sources * 2 * per_dst
    return pl.pallas_call(
        functools.partial(dispatch_kernel, top=top, per_dst=per_dst),
        out_shape=(
            jax.ShapeDtypeStruct((dsts, slots, wide), BF16),
            jax.ShapeDtypeStruct((sources // 2, dsts * 4 * per_dst, 2 * queries), BF16),
        ),
        in_specs=[pl.BlockSpec(memory_space=pltpu.SMEM), pl.BlockSpec(memory_space=pltpu.VMEM)],
        out_specs=[pl.BlockSpec(memory_space=pltpu.VMEM)] * 2,
        compiler_params=pltpu.CompilerParams(vmem_limit_bytes=VMEM_LIMIT),
        name="dispatch",
    )(grp, x)


def score_kernel(count_ref, x_ref, w_ref, ret_ref, grad_ref, *, per_dst):
    devs, slots, wide = x_ref.shape
    all_labels, width = w_ref.shape
    labels = all_labels // per_dst
    rows = devs * slots
    x = x_ref[...].reshape(rows, wide)
    want = x[:, width:].astype(F32)
    scores = lax.dot_general(
        x[:, 0:width], w_ref[...], (((1,), (1,)), ((), ())), preferred_element_type=F32
    )
    own = iota((rows, labels), 0) % per_dst
    label = iota((rows, labels), 1)
    s = scores[:, 0:labels]
    count = jnp.full((rows, labels), count_ref[0], jnp.int32)
    for cl in range(1, per_dst):
        s = jnp.where(own == cl, scores[:, cl * labels : (cl + 1) * labels], s)
        count = jnp.where(own == cl, count_ref[cl], count)
    valid = label < count
    target = (label.astype(F32) + 1.0) == want
    small = jnp.exp(-jnp.abs(s))
    soft = jnp.maximum(s, 0.0) + jnp.log1p(small)
    term = jnp.where(valid, soft - jnp.where(target, s, 0.0), 0.0)
    loss = jnp.sum(term, axis=1, keepdims=True)
    sig = jnp.where(s >= 0.0, 1.0, small) / (1.0 + small)
    grad = jnp.where(valid, sig - jnp.where(target, 1.0, 0.0), 0.0)
    wide_grad = jnp.concatenate(
        [jnp.where(own == cl, grad, 0.0) for cl in range(per_dst)], axis=1
    ).astype(BF16)
    grad_ref[...] = wide_grad
    part = jnp.dot(wide_grad, w_ref[...], preferred_element_type=F32).astype(BF16)
    ret_ref[:, :, 0:width] = part.reshape(devs, slots, width)
    ret_ref[:, :, width:] = (
        jnp.broadcast_to(loss, (rows, EXTRA)).astype(BF16).reshape(devs, slots, EXTRA)
    )


def score(x, weights, count, block):
    devs, slots, wide = x.shape
    per_dst = count.shape[0]
    all_labels, width = weights.shape
    return pl.pallas_call(
        functools.partial(score_kernel, per_dst=per_dst),
        grid=(devs // block,),
        out_shape=(
            jax.ShapeDtypeStruct((devs, slots, wide), BF16),
            jax.ShapeDtypeStruct((devs * slots, all_labels), BF16),
        ),
        in_specs=[
            pl.BlockSpec(memory_space=pltpu.SMEM),
            pl.BlockSpec((block, slots, wide), lambda i: (i, 0, 0)),
            pl.BlockSpec((all_labels, width), lambda i: (0, 0)),
        ],
        out_specs=[
            pl.BlockSpec((block, slots, wide), lambda i: (i, 0, 0)),
            pl.BlockSpec((block * slots, all_labels), lambda i: (i, 0)),
        ],
        compiler_params=pltpu.CompilerParams(vmem_limit_bytes=VMEM_LIMIT),
        name="score",
    )(count, x, weights)


def weight_kernel(x_ref, grad_ref, out_ref, *, width):
    devs, slots, wide = x_ref.shape
    x = x_ref[...].reshape(devs * slots, wide)[:, 0:width]
    part = lax.dot_general(
        grad_ref[...], x, (((0,), (0,)), ((), ())), preferred_element_type=F32
    )

    @pl.when(pl.program_id(0) == 0)
    def _():
        out_ref[...] = part

    @pl.when(pl.program_id(0) > 0)
    def _():
        out_ref[...] += part


def weight_gradient(x, grad, width, block):
    devs, slots, wide = x.shape
    all_labels = grad.shape[1]
    return pl.pallas_call(
        functools.partial(weight_kernel, width=width),
        grid=(devs // block,),
        out_shape=jax.ShapeDtypeStruct((all_labels, width), F32),
        in_specs=[
            pl.BlockSpec((block, slots, wide), lambda i: (i, 0, 0)),
            pl.BlockSpec((block * slots, all_labels), lambda i: (i, 0)),
        ],
        out_specs=pl.BlockSpec((all_labels, width), lambda i: (0, 0)),
        compiler_params=pltpu.CompilerParams(vmem_limit_bytes=VMEM_LIMIT),
        cost_estimate=pl.CostEstimate(
            flops=2 * devs * slots * all_labels * width,
            bytes_accessed=2 * devs * slots * (wide + all_labels) + 4 * all_labels * width,
            transcendentals=0,
        ),
        name="weight_gradient",
    )(x, grad)


def combine_kernel(ret_ref, pick_ref, out_ref):
    pairs, rows, _ = pick_ref.shape
    dsts, _, wide = ret_ref.shape
    two = rows // dsts
    for pair in range(pairs):
        x = ret_ref[:, pl.ds(pair * two, two), :].reshape(rows, wide)
        out = lax.dot_general(
            pick_ref[pair], x, (((0,), (0,)), ((), ())), preferred_element_type=F32
        )
        out_ref[pair] = out.astype(BF16)


def combine(ret, pick):
    pairs, rows, queries = pick.shape
    wide = ret.shape[2]
    return pl.pallas_call(
        combine_kernel,
        out_shape=jax.ShapeDtypeStruct((pairs, queries, wide), BF16),
        in_specs=[pl.BlockSpec(memory_space=pltpu.VMEM)] * 2,
        out_specs=pl.BlockSpec(memory_space=pltpu.VMEM),
        compiler_params=pltpu.CompilerParams(vmem_limit_bytes=VMEM_LIMIT),
        name="combine",
    )(ret, pick)


def per_device(encodings, label_weights, label_count, matched, positive):
    queries, width = encodings.shape
    top = matched.shape[1]
    per_dst = label_count.shape[0]
    dsts = lax.axis_size("dev")
    groups = lax.axis_size("grp")
    in_group = per_dst * dsts
    labels = label_weights.shape[0] // per_dst
    meta = jnp.concatenate([matched // in_group, matched % in_group, positive], axis=1).astype(BF16)
    meta = jnp.pad(meta, ((0, 0), (0, EXTRA - 3 * top)))
    own = jnp.concatenate([encodings, meta], axis=1)
    gathered = lax.all_gather(own, "grp", axis=0, tiled=False)
    me = lax.axis_index("grp").astype(jnp.int32).reshape(1)
    send, pick = dispatch(gathered, me, dsts, per_dst, top)
    received = lax.all_to_all(send, "dev", split_axis=0, concat_axis=0, tiled=True)
    part, grad = score(received, label_weights, label_count, min(8, dsts))
    returned = lax.all_to_all(part, "dev", split_axis=0, concat_axis=0, tiled=True)
    weight_grad = weight_gradient(received, grad, width, min(8, dsts))
    partial = combine(returned, pick).reshape(groups * queries, width + EXTRA)
    total = lax.psum_scatter(partial, "grp", scatter_dimension=0, tiled=True)
    enc_grad = total[:, 0:width]
    query_loss = total[:, width].astype(F32) / (top * labels)
    return enc_grad, query_loss, weight_grad


def solution(mesh):
    in_specs = (
        P(("grp", "dev"), None),
        P(("grp", "dev"), None),
        P(("grp", "dev")),
        P(("grp", "dev"), None),
        P(("grp", "dev"), None),
    )
    out_specs = (P(("grp", "dev"), None), P(("grp", "dev")), P(("grp", "dev"), None))
    return jax.shard_map(
        per_device, mesh=mesh, in_specs=in_specs, out_specs=out_specs, check_vma=False
    )
```

```python
import functools

import jax
import jax.numpy as jnp
from jax import lax
from jax.experimental import pallas as pl
from jax.experimental.pallas import tpu as pltpu
from jax.sharding import PartitionSpec as P

F32 = jnp.float32
BF16 = jnp.bfloat16
LANES = 128
TILE = 8
META = 16
PARAMS = pltpu.CompilerParams(vmem_limit_bytes=63 * 1024 * 1024)
SMALL = pltpu.CompilerParams(vmem_limit_bytes=28 * 1024 * 1024)
IN_HBM = pl.BlockSpec(memory_space=pltpu.HBM)
IN_VMEM = pl.BlockSpec(memory_space=pltpu.VMEM)


def iota(shape, dim):
    return lax.broadcasted_iota(jnp.int32, shape, dim)


def whole(shape):
    return pl.BlockSpec(shape, lambda i: (0,) * len(shape))


def unit_row(row):
    return (iota((LANES, LANES), 0) == row).astype(BF16)


def unit_column(shape, column):
    return (iota(shape, 1) == column).astype(BF16)


def store_tiles(ref, first, rows, at=slice(None)):
    for k in range(0, rows.shape[2] // LANES, 2):
        left = rows[:, :, k * LANES : (k + 1) * LANES]
        right = rows[:, :, (k + 1) * LANES : (k + 2) * LANES]
        ref[at, pl.ds(first + k * TILE, 2 * TILE), :] = jnp.concatenate([left, right], axis=1).astype(BF16)


def load_tiles(held, width):
    devs, tile_rows, _ = held.shape
    per_source = width // LANES
    sources = (tile_rows // TILE - 1) // per_source
    tiles = held.astype(F32).reshape(devs, tile_rows // TILE, TILE, LANES)
    rows = [
        jnp.concatenate([tiles[:, s * per_source + k] for k in range(per_source)], axis=2)
        for s in range(sources)
    ]
    return rows, tiles[:, sources * per_source].reshape(devs * TILE, LANES).astype(BF16)


def prepare_kernel(enc_ref, matched_ref, positive_ref, out_ref, held, sems, *, in_group):
    queries = enc_ref.shape[0]
    top = matched_ref.shape[0]
    copies = [
        pltpu.make_async_copy(matched_ref, held.at[0], sems.at[0]),
        pltpu.make_async_copy(positive_ref, held.at[1], sems.at[1]),
        pltpu.make_async_copy(enc_ref, out_ref.at[pl.ds(0, queries)], sems.at[2]),
    ]
    for copy in copies:
        copy.start()
    copies[0].wait()
    copies[1].wait()
    matched = held[0]
    group = matched // in_group
    parts = (group, matched - group * in_group, held[1])
    meta = jnp.concatenate([part.astype(F32) for part in parts], axis=1)
    meta = jnp.concatenate([meta, jnp.zeros((top, out_ref.shape[1] - meta.shape[1]), F32)], axis=1)
    meta = jnp.concatenate([meta, jnp.zeros((META - top, meta.shape[1]), F32)], axis=0)
    out_ref[queries:] = meta.astype(BF16)
    copies[2].wait()


def prepare(encodings, matched, positive, in_group):
    queries, width = encodings.shape
    top = matched.shape[1]
    return pl.pallas_call(
        functools.partial(prepare_kernel, in_group=in_group),
        out_shape=jax.ShapeDtypeStruct((queries + META, width), BF16),
        in_specs=[IN_HBM] * 3,
        out_specs=IN_VMEM,
        scratch_shapes=[pltpu.VMEM((2, top, queries), jnp.int32), pltpu.SemaphoreType.DMA((3,))],
        compiler_params=PARAMS,
        name="prepare",
    )(encodings, matched.T, positive.T)


def dispatch_kernel(grp_ref, *refs, parts, top, per_dst, steps):
    x_refs, (send_ref, pick_ref, send, picks, sems) = refs[:-5], refs[-5:]
    width = x_refs[0].shape[1]
    queries = pick_ref.shape[2]
    sources = len(parts)
    dsts = send_ref.shape[0] // steps
    rows = dsts * TILE
    me = grp_ref[0].astype(F32)
    row = iota((rows, queries), 0)
    rank = ((row // per_dst) % 2).astype(F32)
    before = (iota((queries, queries), 0) < iota((queries, queries), 1)).astype(BF16)
    blocks, keys, wants, first = [], [], [], 0
    for count in parts:
        x = jnp.concatenate([r[...] for r in x_refs[first : first + count]], axis=0)
        first += count
        meta = x[queries:].astype(F32)[0:top]
        group, local, slot = [meta[:, i * queries : (i + 1) * queries] for i in range(3)]
        blocks.append(x[0:queries])
        keys.append(jnp.where(group == me, local, -1.0).astype(BF16))
        wants.append((slot + 1.0).astype(BF16))
    copies = []
    for step in range(steps):
        cluster = ((row // TILE + step * dsts) * per_dst + row % per_dst).astype(F32).astype(BF16)
        at, at_rows = pl.ds(step * dsts, dsts), pl.ds(step * rows, rows)
        last = jnp.zeros((rows, LANES), F32)
        for source in range(sources):
            value = jnp.zeros((rows, queries), BF16)
            for t in range(top):
                same = cluster == keys[source][t : t + 1]
                value = value + jnp.where(same, wants[source][t : t + 1], jnp.zeros((), BF16))
            hit = (value > 0.0).astype(BF16)
            earlier = jnp.dot(hit, before, preferred_element_type=F32)
            value = jnp.where(earlier == rank, value.astype(F32), 0.0)
            pick = (value > 0.0).astype(BF16)
            picks[source, at_rows, :] = pick
            out = jnp.dot(pick, blocks[source], preferred_element_type=F32)
            store_tiles(send, source * width // LANES * TILE, out.reshape(dsts, TILE, width), at)
            place = unit_column((queries, LANES), source)
            last = last + jnp.dot(value.astype(BF16), place, preferred_element_type=F32)
        end = sources * width // LANES * TILE
        send[at, end:, :] = last.reshape(dsts, TILE, LANES).astype(BF16)
        copies.append(pltpu.make_async_copy(send.at[at], send_ref.at[at], sems.at[0, step]))
        copies.append(
            pltpu.make_async_copy(picks.at[:, at_rows], pick_ref.at[:, at_rows], sems.at[1, step])
        )
        copies[-2].start()
        copies[-1].start()
    for copy in copies:
        copy.wait()


def dispatch(sources, grp, dsts, per_dst, top):
    flat = [block for blocks in sources for block in blocks]
    queries = sum(block.shape[0] for block in sources[0]) - META
    width = flat[0].shape[1]
    send = (dsts, (len(sources) * width // LANES + 1) * TILE, LANES)
    pick = (len(sources), dsts * TILE, queries)
    steps = 2
    return pl.pallas_call(
        functools.partial(
            dispatch_kernel,
            parts=[len(blocks) for blocks in sources],
            top=top,
            per_dst=per_dst,
            steps=steps,
        ),
        out_shape=(jax.ShapeDtypeStruct(send, BF16), jax.ShapeDtypeStruct(pick, BF16)),
        in_specs=[pl.BlockSpec(memory_space=pltpu.SMEM)] + [IN_VMEM] * len(flat),
        out_specs=[IN_HBM, IN_HBM],
        scratch_shapes=[
            pltpu.VMEM(send, BF16),
            pltpu.VMEM(pick, BF16),
            pltpu.SemaphoreType.DMA((2, steps)),
        ],
        compiler_params=SMALL,
        name="dispatch",
    )(grp, *flat)


def own_columns(grad, per_dst):
    own = iota(grad.shape, 0) % per_dst
    return jnp.concatenate([jnp.where(own == cl, grad, 0.0) for cl in range(per_dst)], axis=1).astype(BF16)


def score_kernel(count_ref, x_ref, w_ref, *refs, per_dst, carried, outs):
    carry_ref, ret_refs, grad_ref = refs[0], refs[1 if carried else 0 : -1], refs[-1]
    devs = x_ref.shape[0]
    all_labels, width = w_ref.shape
    labels = all_labels // per_dst
    per_source = width // LANES * TILE
    tiles, last = load_tiles(x_ref[...], width)
    sources = len(tiles)
    rows = devs * sources * TILE
    x = jnp.concatenate([t.reshape(devs, 1, TILE, width) for t in tiles], axis=1)
    x = x.reshape(rows, width).astype(BF16)
    want = jnp.concatenate(
        [
            jnp.dot(last, unit_row(s), preferred_element_type=F32).reshape(devs, 1, TILE, LANES)
            for s in range(sources)
        ],
        axis=1,
    ).reshape(rows, LANES)
    scores = lax.dot_general(
        x, w_ref[...], (((1,), (1,)), ((), ())), preferred_element_type=F32
    )
    own = iota((rows, labels), 0) % per_dst
    label = iota((rows, labels), 1)
    s = scores[:, 0:labels]
    count = jnp.full((rows, labels), count_ref[0], jnp.int32)
    for cl in range(1, per_dst):
        s = jnp.where(own == cl, scores[:, cl * labels : (cl + 1) * labels], s)
        count = jnp.where(own == cl, count_ref[cl], count)
    valid = label < count
    target = (label.astype(F32) + 1.0) == want
    small = jnp.exp(-jnp.abs(s))
    soft = jnp.maximum(s, 0.0) + jnp.log(1.0 + small)
    term = jnp.where(valid, soft - jnp.where(target, s, 0.0), 0.0)
    loss = jnp.sum(term, axis=1, keepdims=True).reshape(devs, sources, TILE, 1)
    sig = jnp.where(s >= 0.0, 1.0, small) / (1.0 + small)
    grad = jnp.where(valid, sig - jnp.where(target, 1.0, 0.0), 0.0)
    grad_ref[...] = grad.astype(BF16)
    part = jnp.dot(own_columns(grad, per_dst), w_ref[...], preferred_element_type=F32)
    part = part.reshape(devs, sources, TILE, width)
    lane = iota((devs, TILE, LANES), 2)
    for i, (ret_ref, members) in enumerate(zip(ret_refs, outs)):
        before = carried if i == 0 else 0
        last = jnp.zeros((devs, TILE, LANES), F32)
        if before:
            end = before * per_source
            ret_ref[:, 0:end, :] = carry_ref[:, 0:end, :]
            last = carry_ref[:, end:, :].astype(F32)
        for j, source in enumerate(members):
            store_tiles(ret_ref, (before + j) * per_source, part[:, source])
            last = jnp.where(lane == before + j, loss[:, source], last)
        ret_ref[:, (before + len(members)) * per_source :, :] = last.astype(BF16)


def sources_of(x, width):
    return (x.shape[1] // TILE - 1) * LANES // width


def score(x, weights, count, block, outs, carry=None):
    devs, tile_rows, _ = x.shape
    per_dst = count.shape[0]
    all_labels, width = weights.shape
    labels = all_labels // per_dst
    slots = sources_of(x, width) * TILE
    carried = sources_of(carry, width) if carry is not None else 0
    sizes = [len(members) + (carried if i == 0 else 0) for i, members in enumerate(outs)]
    ret_rows = [(size * width // LANES + 1) * TILE for size in sizes]

    def by_dev(rows):
        return pl.BlockSpec((block, rows, LANES), lambda i: (i, 0, 0))

    return pl.pallas_call(
        functools.partial(score_kernel, per_dst=per_dst, carried=carried, outs=outs),
        grid=(devs // block,),
        out_shape=[jax.ShapeDtypeStruct((devs, r, LANES), BF16) for r in ret_rows]
        + [jax.ShapeDtypeStruct((devs * slots, labels), BF16)],
        in_specs=[
            pl.BlockSpec(memory_space=pltpu.SMEM),
            by_dev(tile_rows),
            whole((all_labels, width)),
        ]
        + ([by_dev(carry.shape[1])] if carried else []),
        out_specs=[by_dev(r) for r in ret_rows]
        + [pl.BlockSpec((block * slots, labels), lambda i: (i, 0))],
        compiler_params=PARAMS,
        cost_estimate=pl.CostEstimate(
            flops=4 * devs * slots * all_labels * width,
            bytes_accessed=4 * devs * slots * (width + labels) + 2 * all_labels * width,
            transcendentals=0,
        ),
        name="score",
    )(count, x, weights, *([carry] if carried else []))


def weight_kernel(*refs, per_dst):
    out_ref = refs[-1]
    width = out_ref.shape[1]
    total = None
    for x_ref, grad_ref in zip(refs[0:-1:2], refs[1:-1:2]):
        tiles, _ = load_tiles(x_ref[...], width)
        devs = x_ref.shape[0]
        x = jnp.concatenate([t.reshape(devs, 1, TILE, width) for t in tiles], axis=1)
        x = x.reshape(devs * len(tiles) * TILE, width).astype(BF16)
        grad = own_columns(grad_ref[...].astype(F32), per_dst)
        part = lax.dot_general(
            grad, x, (((0,), (0,)), ((), ())), preferred_element_type=F32
        )
        total = part if total is None else total + part

    @pl.when(pl.program_id(0) == 0)
    def _():
        out_ref[...] = total

    @pl.when(pl.program_id(0) > 0)
    def _():
        out_ref[...] += total


def weight_gradient(chunks, width, block, per_dst):
    labels = chunks[0][1].shape[1]
    all_labels = labels * per_dst
    devs = chunks[0][0].shape[0]
    rows = sum(grad.shape[0] for _, grad in chunks)
    flat = [a for chunk in chunks for a in chunk]
    specs = []
    for x, grad in chunks:
        specs.append(pl.BlockSpec((block,) + x.shape[1:], lambda i: (i, 0, 0)))
        specs.append(pl.BlockSpec((grad.shape[0] * block // devs, labels), lambda i: (i, 0)))
    return pl.pallas_call(
        functools.partial(weight_kernel, per_dst=per_dst),
        grid=(devs // block,),
        out_shape=jax.ShapeDtypeStruct((all_labels, width), F32),
        in_specs=specs,
        out_specs=whole((all_labels, width)),
        compiler_params=PARAMS,
        cost_estimate=pl.CostEstimate(
            flops=2 * rows * all_labels * width,
            bytes_accessed=2 * rows * (width + all_labels) + 4 * all_labels * width,
            transcendentals=0,
        ),
        name="weight_gradient",
    )(*flat)


def combine_kernel(ret_ref, *refs, order, picks, parts, added, width, steps):
    pick_refs, refs = refs[:picks], refs[picks:]
    add_refs, refs = dict(zip(added, refs[: len(added)])), refs[len(added) :]
    out_refs, ret = refs[: sum(parts)], refs[sum(parts)]
    held, sems = refs[sum(parts) + 1 : -1], refs[-1]
    dsts = ret_ref.shape[0] // steps
    queries = held[0].shape[2]
    rows = dsts * TILE
    over_rows = (((0,), (0,)), ((), ()))
    ats = [pl.ds(step * dsts, dsts) for step in range(steps)]
    pick_copies = [
        pltpu.make_async_copy(ref, place, sems.at[steps + i])
        for i, (ref, place) in enumerate(zip(pick_refs, held))
    ]
    ret_copies = [
        pltpu.make_async_copy(ret_ref.at[at], ret.at[at], sems.at[step]) for step, at in enumerate(ats)
    ]
    for copy in pick_copies + ret_copies:
        copy.start()
    for copy in pick_copies:
        copy.wait()
    totals = [None] * len(order)
    for step, at in enumerate(ats):
        ret_copies[step].wait()
        tiles, last = load_tiles(ret[at], width)
        for source, (which, index) in enumerate(order):
            pick = held[which][index, pl.ds(step * rows, rows), :]
            x = tiles[source].reshape(rows, width).astype(BF16)
            loss = jnp.dot(last, unit_row(source), preferred_element_type=F32).astype(BF16)
            x = jnp.concatenate([x, loss], axis=1)
            out = lax.dot_general(pick, x, over_rows, preferred_element_type=F32)
            totals[source] = out if step == 0 else totals[source] + out
    first = 0
    for source, count in enumerate(parts):
        out = totals[source]
        if source in add_refs:
            out = out + add_refs[source][...].astype(F32)
        part = queries // count
        for i in range(count):
            out_refs[first + i][...] = out[i * part : (i + 1) * part].astype(BF16)
        first += count


def combine(ret, picks, order, parts, width, arrived=(), params=SMALL):
    queries = picks[0].shape[2]
    shapes = [(queries // count, width + LANES) for count in parts for _ in range(count)]
    added = [a for _, a in arrived]
    steps = 2
    return pl.pallas_call(
        functools.partial(
            combine_kernel,
            order=order,
            picks=len(picks),
            parts=parts,
            added=[i for i, _ in arrived],
            width=width,
            steps=steps,
        ),
        out_shape=[jax.ShapeDtypeStruct(shape, BF16) for shape in shapes],
        in_specs=[IN_HBM] * (1 + len(picks)) + [IN_VMEM] * len(added),
        out_specs=[IN_VMEM] * len(shapes),
        scratch_shapes=[pltpu.VMEM(ret.shape, BF16)]
        + [pltpu.VMEM(pick.shape, BF16) for pick in picks]
        + [pltpu.SemaphoreType.DMA((steps + len(picks),))],
        compiler_params=params,
        name="combine",
    )(ret, *picks, *added)


def add(a, b):
    return (a.astype(F32) + b.astype(F32)).astype(BF16)


def add_half(a, half, second):
    zero = jnp.zeros_like(half)
    return add(a, jnp.concatenate([zero, half] if second else [half, zero], axis=0))


def per_device(encodings, label_weights, label_count, matched, positive):
    queries, width = encodings.shape
    top = matched.shape[1]
    per_dst = label_count.shape[0]
    dsts = lax.axis_size("dev")
    groups = lax.axis_size("grp")
    labels = label_weights.shape[0] // per_dst
    half = queries // 2
    reach = groups // 2
    up_pairs = [(i, (i + 1) % groups) for i in range(groups)]
    down_pairs = [(i, (i - 1) % groups) for i in range(groups)]

    def up(v):
        return lax.ppermute(v, "grp", up_pairs)

    def down(v):
        return lax.ppermute(v, "grp", down_pairs)

    def exchange(v):
        return lax.all_to_all(v, "dev", split_axis=0, concat_axis=0, tiled=True)

    me = lax.axis_index("grp").astype(jnp.int32).reshape(1)
    own = prepare(encodings, matched, positive, per_dst * dsts)
    lower, upper = [own], [own]
    for _ in range(1, reach):
        lower.append(up(lower[-1]))
        upper.append(down(upper[-1]))
    across = (up(lower[-1][:half]), down(upper[-1][half:]))
    chunks = [
        [(own,)],
        [(v[k],) for k in range(1, reach - 1) for v in (lower, upper)],
        [(lower[-1],), (upper[-1],), across],
    ]
    picks, got = [], []
    for sources in chunks:
        send, pick = dispatch(sources, me, dsts, per_dst, top)
        if got:
            send, got[-1] = lax.optimization_barrier((send, got[-1]))
        got.append(exchange(send))
        picks.append(pick)

    block = min(16, dsts)
    mid = list(range(len(chunks[1])))
    part_own, grad_own = score(got[0], label_weights, label_count, block, [[0]])
    part_near, part_mid, grad_mid = score(
        got[1], label_weights, label_count, block, [mid[:2], mid[2:]], part_own
    )
    part_mid, part_near = lax.optimization_barrier((part_mid, part_near))
    part_far, grad_far = score(got[2], label_weights, label_count, block, [[0, 1, 2]], part_mid)
    back_far = exchange(part_far)
    weight_grad = weight_gradient(list(zip(got, [grad_own, grad_mid, grad_far])), width, block, per_dst)
    part_near, back_far, weight_grad = lax.optimization_barrier((part_near, back_far, weight_grad))
    back_near = exchange(part_near)

    order = [(0, i) for i in mid[2:]] + [(1, 0), (1, 1), (1, 2)]
    parts = [1] * (len(order) - 1) + [2]
    sums = list(combine(back_far, picks[1:], order, parts, width, (), PARAMS))
    to_lower, to_upper = down(sums[-2]), up(sums[-1])
    sums = sums[:-2]
    sums[-2:] = [add_half(sums[-2], to_lower, False), add_half(sums[-1], to_upper, True)]
    to_lower, to_upper = down(sums[-2]), up(sums[-1])
    sums = sums[:-2]
    while sums:
        to_lower, to_upper = down(add(sums[-2], to_lower)), up(add(sums[-1], to_upper))
        sums = sums[:-2]
    order = [(0, 0), (1, 0), (1, 1)]
    arrived = ((1, to_lower), (2, to_upper))
    mine, a, b = combine(back_near, picks[:2], order, [1, 1, 1], width, arrived)
    to_lower, to_upper = down(a), up(b)
    total = mine.astype(F32) + to_lower.astype(F32) + to_upper.astype(F32)
    enc_grad = total[:, 0:width].astype(BF16)
    query_loss = total[:, width] / (top * labels)
    return enc_grad, query_loss, weight_grad


def solution(mesh):
    in_specs = (
        P(("grp", "dev"), None),
        P(("grp", "dev"), None),
        P(("grp", "dev")),
        P(("grp", "dev"), None),
        P(("grp", "dev"), None),
    )
    out_specs = (P(("grp", "dev"), None), P(("grp", "dev")), P(("grp", "dev"), None))
    return jax.shard_map(
        per_device, mesh=mesh, in_specs=in_specs, out_specs=out_specs, check_vma=False
    )
```

```python
import functools

import jax
import jax.numpy as jnp
from jax import lax
from jax.experimental import pallas as pl
from jax.experimental.pallas import tpu as pltpu
from jax.sharding import PartitionSpec as P

F32 = jnp.float32
BF16 = jnp.bfloat16
LANES = 128
TILE = 8
META = 16
PARAMS = pltpu.CompilerParams(vmem_limit_bytes=63 * 1024 * 1024)
SMALL = pltpu.CompilerParams(vmem_limit_bytes=28 * 1024 * 1024)
IN_HBM = pl.BlockSpec(memory_space=pltpu.HBM)
IN_VMEM = pl.BlockSpec(memory_space=pltpu.VMEM)

SLOTS = TILE - 1
MOVED = 128


def iota(shape, dim):
    return lax.broadcasted_iota(jnp.int32, shape, dim)


def whole(shape):
    return pl.BlockSpec(shape, lambda i: (0,) * len(shape))


def unit_row(row):
    return (iota((LANES, LANES), 0) == row).astype(BF16)


def unit_column(shape, column):
    return (iota(shape, 1) == column).astype(BF16)


def to_tiles(rows):
    tiles = [rows[:, :, k * LANES : (k + 1) * LANES] for k in range(TILE)]
    under = iota(tiles[0].shape, 1) == SLOTS
    return [jnp.where(under, tiles[SLOTS][:, k : k + 1], tiles[k]) for k in range(SLOTS)]


def store_tiles(ref, at, tiles):
    for k in range(0, len(tiles), 2):
        pair = jnp.concatenate(tiles[k : k + 2], axis=1)
        ref[at, k * TILE : k * TILE + pair.shape[1], :] = pair.astype(BF16)


def load_tiles(held):
    devs, tile_rows, _ = held.shape
    tiles = held.astype(F32).reshape(devs, tile_rows // TILE, TILE, LANES)
    sublane = iota((devs, TILE, LANES), 1)
    rows = []
    for s in range(tile_rows // TILE // SLOTS):
        own = [tiles[:, s * SLOTS + k] for k in range(SLOTS)]
        end = own[0][:, SLOTS : SLOTS + 1]
        for k in range(1, SLOTS):
            end = jnp.where(sublane == k, own[k][:, SLOTS : SLOTS + 1], end)
        rows.append(jnp.concatenate(own + [jnp.broadcast_to(end, own[0].shape)], axis=2))
    return rows, tiles[:, -1].reshape(devs * TILE, LANES).astype(BF16)


def sources_of(x):
    return (x.shape[1] // TILE - 1) // SLOTS


def tile_rows_of(sources):
    return (sources * SLOTS + 1) * TILE


def wanted(last, sources, devs):
    parts = [
        jnp.dot(last, unit_row(s), preferred_element_type=F32).reshape(devs, 1, TILE, LANES)
        for s in range(sources)
    ]
    return jnp.concatenate(parts, axis=1).reshape(devs * sources * TILE, LANES)


def own_cluster(want, per_dst):
    place = iota(want.shape, 0) % per_dst
    return jnp.where(want > MOVED, per_dst - 1, place)


def prepare_kernel(
    enc_ref, matched_ref, positive_ref, out_ref, held, sems, *, in_group, per_dst, receivers
):
    queries = enc_ref.shape[0]
    top = matched_ref.shape[0]
    copies = [
        pltpu.make_async_copy(matched_ref, held.at[0], sems.at[0]),
        pltpu.make_async_copy(positive_ref, held.at[1], sems.at[1]),
        pltpu.make_async_copy(enc_ref, out_ref.at[pl.ds(0, queries)], sems.at[2]),
    ]
    for copy in copies:
        copy.start()
    copies[0].wait()
    copies[1].wait()
    matched = held[0]
    group = matched // in_group
    parts = (group, matched - group * in_group, held[1])
    meta = jnp.concatenate([part.astype(F32) for part in parts], axis=1)
    meta = jnp.concatenate([meta, jnp.zeros((top, out_ref.shape[1] - meta.shape[1]), F32)], axis=1)
    receiver = matched // per_dst
    receivers = iota((receivers, queries), 0)
    load = jnp.zeros(receivers.shape, F32)
    for t in range(top):
        load = load + (receivers == receiver[t : t + 1]).astype(F32)
    load = jnp.max(jnp.sum(load, axis=1, keepdims=True), axis=0, keepdims=True)
    over = jnp.broadcast_to(jnp.where(load > SLOTS, 1.0, 0.0), (META - top, meta.shape[1]))
    meta = jnp.concatenate([meta, over], axis=0)
    out_ref[queries:] = meta.astype(BF16)
    copies[2].wait()


def prepare(encodings, matched, positive, in_group, per_dst, receivers):
    queries, width = encodings.shape
    top = matched.shape[1]
    return pl.pallas_call(
        functools.partial(
            prepare_kernel, in_group=in_group, per_dst=per_dst, receivers=receivers
        ),
        out_shape=jax.ShapeDtypeStruct((queries + META, width), BF16),
        in_specs=[IN_HBM] * 3,
        out_specs=IN_VMEM,
        scratch_shapes=[pltpu.VMEM((2, top, queries), jnp.int32), pltpu.SemaphoreType.DMA((3,))],
        compiler_params=PARAMS,
        name="prepare",
    )(encodings, matched.T, positive.T)


def dispatch_kernel(grp_ref, *refs, parts, top, per_dst, steps):
    x_refs, (seen_ref, send_ref, pick_ref, now_ref, send, picks, sems) = refs[:-7], refs[-7:]
    width = x_refs[0].shape[1]
    queries = pick_ref.shape[2]
    sources = len(parts)
    dsts = send_ref.shape[0] // steps
    rows = dsts * TILE
    me = grp_ref[0].astype(F32)
    row = iota((rows, queries), 0)
    rank = ((row // per_dst) % 2).astype(F32)
    before = (iota((queries, queries), 0) < iota((queries, queries), 1)).astype(BF16)
    blocks, keys, wants, first = [], [], [], 0
    seen = seen_ref[...]
    for count in parts:
        x = jnp.concatenate([r[...] for r in x_refs[first : first + count]], axis=0)
        first += count
        meta = x[queries:].astype(F32)[0:top]
        group, local, slot = [meta[:, i * queries : (i + 1) * queries] for i in range(3)]
        blocks.append(x[0:queries])
        seen = jnp.maximum(seen, x[queries:].astype(F32)[TILE : 2 * TILE, 0:LANES])
        keys.append(jnp.where(group == me, local, -1.0).astype(BF16))
        wants.append((slot + 1.0).astype(BF16))
    now_ref[...] = seen
    ones = jnp.ones((queries, LANES), BF16)
    copies = []
    for step in range(steps):
        cluster = ((row // TILE + step * dsts) * per_dst + row % per_dst).astype(F32).astype(BF16)
        at, at_rows = pl.ds(step * dsts, dsts), pl.ds(step * rows, rows)
        lane = iota((dsts, TILE, LANES), 2)
        sublane = iota((dsts, TILE, LANES), 1)
        last = jnp.where(lane == LANES - 1, jnp.broadcast_to(seen, lane.shape), 0.0)
        tiles = []
        for source in range(sources):
            value = jnp.zeros((rows, queries), BF16)
            for t in range(top):
                same = cluster == keys[source][t : t + 1]
                value = value + jnp.where(same, wants[source][t : t + 1], jnp.zeros((), BF16))
            hit = (value > 0.0).astype(BF16)
            earlier = jnp.dot(hit, before, preferred_element_type=F32)
            value = jnp.where(earlier == rank, value.astype(F32), 0.0)
            want = jnp.dot(value.astype(BF16), ones, preferred_element_type=F32)
            value = value.reshape(dsts, TILE, queries)
            want = want.reshape(dsts, TILE, LANES)
            value_end, want_end = value[:, SLOTS : SLOTS + 1], want[:, SLOTS : SLOTS + 1]
            waiting = want_end > 0.0
            for slot in range(per_dst, SLOTS):
                free = want[:, slot : slot + 1] == 0.0
                here = (sublane == slot) & jnp.broadcast_to(waiting & free, sublane.shape)
                value = jnp.where(here, value_end, value)
                want = jnp.where(here, want_end + MOVED, want)
                waiting = waiting & jnp.logical_not(free)
            value = jnp.where(sublane == SLOTS, 0.0, value)
            want = jnp.where(sublane == SLOTS, 0.0, want)
            pick = (value > 0.0).astype(F32).reshape(rows, queries).astype(BF16)
            picks[source, at_rows, :] = pick
            out = jnp.dot(pick, blocks[source], preferred_element_type=F32)
            tiles.extend(to_tiles(out.reshape(dsts, TILE, width)))
            last = jnp.where(lane == source, want, last)
        store_tiles(send, at, tiles + [last])
        copies.append(pltpu.make_async_copy(send.at[at], send_ref.at[at], sems.at[0, step]))
        copies.append(
            pltpu.make_async_copy(picks.at[:, at_rows], pick_ref.at[:, at_rows], sems.at[1, step])
        )
        copies[-2].start()
        copies[-1].start()
    for copy in copies:
        copy.wait()


def dispatch(sources, grp, seen, dsts, per_dst, top):
    flat = [block for blocks in sources for block in blocks]
    queries = sum(block.shape[0] for block in sources[0]) - META
    send = (dsts, tile_rows_of(len(sources)), LANES)
    pick = (len(sources), dsts * TILE, queries)
    steps = 2
    return pl.pallas_call(
        functools.partial(
            dispatch_kernel,
            parts=[len(blocks) for blocks in sources],
            top=top,
            per_dst=per_dst,
            steps=steps,
        ),
        out_shape=(
            jax.ShapeDtypeStruct(send, BF16),
            jax.ShapeDtypeStruct(pick, BF16),
            jax.ShapeDtypeStruct((TILE, LANES), F32),
        ),
        in_specs=[pl.BlockSpec(memory_space=pltpu.SMEM)] + [IN_VMEM] * (len(flat) + 1),
        out_specs=[IN_HBM, IN_HBM, IN_VMEM],
        scratch_shapes=[
            pltpu.VMEM(send, BF16),
            pltpu.VMEM(pick, BF16),
            pltpu.SemaphoreType.DMA((2, steps)),
        ],
        compiler_params=SMALL,
        name="dispatch",
    )(grp, *flat, seen)


def own_columns(grad, own, per_dst):
    return jnp.concatenate([jnp.where(own == cl, grad, 0.0) for cl in range(per_dst)], axis=1).astype(BF16)


def score_kernel(count_ref, x_ref, w_ref, *refs, per_dst, carried, outs):
    carry_ref, ret_refs = refs[0], refs[1 if carried else 0 : -2]
    grad_ref, over_ref = refs[-2:]
    devs = x_ref.shape[0]
    all_labels, width = w_ref.shape
    labels = all_labels // per_dst
    tiles, last = load_tiles(x_ref[...])
    sources = len(tiles)
    rows = devs * sources * TILE
    x = jnp.concatenate([t.reshape(devs, 1, TILE, width) for t in tiles], axis=1)
    x = x.reshape(rows, width).astype(BF16)
    want = wanted(last, sources, devs)
    scores = lax.dot_general(
        x, w_ref[...], (((1,), (1,)), ((), ())), preferred_element_type=F32
    )
    own = own_cluster(want, per_dst)
    want = jnp.where(want > MOVED, want - MOVED, want)
    label = iota((rows, labels), 1)
    s = scores[:, 0:labels]
    count = jnp.full((rows, labels), count_ref[0], jnp.int32)
    for cl in range(1, per_dst):
        s = jnp.where(own == cl, scores[:, cl * labels : (cl + 1) * labels], s)
        count = jnp.where(own == cl, count_ref[cl], count)
    valid = (label < count) & (want > 0.0)
    target = (label.astype(F32) + 1.0) == want
    small = jnp.exp(-jnp.abs(s))
    soft = jnp.maximum(s, 0.0) + jnp.log(1.0 + small)
    term = jnp.where(valid, soft - jnp.where(target, s, 0.0), 0.0)
    loss = jnp.sum(term, axis=1, keepdims=True).reshape(devs, sources, TILE, 1)
    sig = jnp.where(s >= 0.0, 1.0, small) / (1.0 + small)
    grad = jnp.where(valid, sig - jnp.where(target, 1.0, 0.0), 0.0)
    grad_ref[...] = grad.astype(BF16)
    part = jnp.dot(own_columns(grad, own, per_dst), w_ref[...], preferred_element_type=F32)
    part = part.reshape(devs, sources, TILE, width)
    lane = iota((devs, TILE, LANES), 2)
    for i, (ret_ref, members) in enumerate(zip(ret_refs, outs)):
        before = carried if i == 0 else 0
        back, end = [], jnp.zeros((devs, TILE, LANES), F32)
        if before:
            carry = carry_ref[...].astype(F32).reshape(devs, before * SLOTS + 1, TILE, LANES)
            back = [carry[:, k] for k in range(before * SLOTS)]
            end = carry[:, before * SLOTS]
        for j, source in enumerate(members):
            back.extend(to_tiles(part[:, source]))
            end = jnp.where(lane == before + j, loss[:, source], end)
        store_tiles(ret_ref, slice(None), back + [end])
    over = jnp.max(last.astype(F32).reshape(devs, TILE, LANES), axis=0)

    @pl.when(pl.program_id(0) == 0)
    def _():
        over_ref[...] = over

    @pl.when(pl.program_id(0) > 0)
    def _():
        over_ref[...] = jnp.maximum(over_ref[...], over)


def score(x, weights, count, block, outs, carry=None):
    devs, tile_rows, _ = x.shape
    per_dst = count.shape[0]
    all_labels, width = weights.shape
    labels = all_labels // per_dst
    slots = sources_of(x) * TILE
    carried = sources_of(carry) if carry is not None else 0
    sizes = [len(members) + (carried if i == 0 else 0) for i, members in enumerate(outs)]
    ret_rows = [tile_rows_of(size) for size in sizes]

    def by_dev(rows):
        return pl.BlockSpec((block, rows, LANES), lambda i: (i, 0, 0))

    return pl.pallas_call(
        functools.partial(score_kernel, per_dst=per_dst, carried=carried, outs=outs),
        grid=(devs // block,),
        out_shape=[jax.ShapeDtypeStruct((devs, r, LANES), BF16) for r in ret_rows]
        + [
            jax.ShapeDtypeStruct((devs * slots, labels), BF16),
            jax.ShapeDtypeStruct((TILE, LANES), F32),
        ],
        in_specs=[
            pl.BlockSpec(memory_space=pltpu.SMEM),
            by_dev(tile_rows),
            whole((all_labels, width)),
        ]
        + ([by_dev(carry.shape[1])] if carried else []),
        out_specs=[by_dev(r) for r in ret_rows]
        + [pl.BlockSpec((block * slots, labels), lambda i: (i, 0)), whole((TILE, LANES))],
        compiler_params=PARAMS,
        cost_estimate=pl.CostEstimate(
            flops=4 * devs * slots * all_labels * width,
            bytes_accessed=4 * devs * slots * (width + labels) + 2 * all_labels * width,
            transcendentals=0,
        ),
        name="score",
    )(count, x, weights, *([carry] if carried else []))


def weight_kernel(*refs, per_dst):
    out_ref = refs[-1]
    width = out_ref.shape[1]
    total = None
    for x_ref, grad_ref in zip(refs[0:-1:2], refs[1:-1:2]):
        tiles, last = load_tiles(x_ref[...])
        devs = x_ref.shape[0]
        own = own_cluster(wanted(last, len(tiles), devs), per_dst)
        x = jnp.concatenate([t.reshape(devs, 1, TILE, width) for t in tiles], axis=1)
        x = x.reshape(devs * len(tiles) * TILE, width).astype(BF16)
        grad = own_columns(grad_ref[...].astype(F32), own, per_dst)
        part = lax.dot_general(
            grad, x, (((0,), (0,)), ((), ())), preferred_element_type=F32
        )
        total = part if total is None else total + part

    @pl.when(pl.program_id(0) == 0)
    def _():
        out_ref[...] = total

    @pl.when(pl.program_id(0) > 0)
    def _():
        out_ref[...] += total


def weight_gradient(chunks, width, block, per_dst):
    labels = chunks[0][1].shape[1]
    all_labels = labels * per_dst
    devs = chunks[0][0].shape[0]
    rows = sum(grad.shape[0] for _, grad in chunks)
    flat = [a for chunk in chunks for a in chunk]
    specs = []
    for x, grad in chunks:
        specs.append(pl.BlockSpec((block,) + x.shape[1:], lambda i: (i, 0, 0)))
        specs.append(pl.BlockSpec((grad.shape[0] * block // devs, labels), lambda i: (i, 0)))
    return pl.pallas_call(
        functools.partial(weight_kernel, per_dst=per_dst),
        grid=(devs // block,),
        out_shape=jax.ShapeDtypeStruct((all_labels, width), F32),
        in_specs=specs,
        out_specs=whole((all_labels, width)),
        compiler_params=PARAMS,
        cost_estimate=pl.CostEstimate(
            flops=2 * rows * all_labels * width,
            bytes_accessed=2 * rows * (width + all_labels) + 4 * all_labels * width,
            transcendentals=0,
        ),
        name="weight_gradient",
    )(*flat)


def combine_kernel(ret_ref, *refs, order, picks, parts, added, base, steps):
    pick_refs, refs = refs[:picks], refs[picks:]
    add_refs, refs = dict(zip(added, refs[: len(added)])), refs[len(added) :]
    out_refs, ret = refs[: sum(parts)], refs[sum(parts)]
    held, sems = refs[sum(parts) + 1 : -1], refs[-1]
    dsts = ret_ref.shape[0] // steps
    queries = held[0].shape[2]
    rows = dsts * TILE
    over_rows = (((0,), (0,)), ((), ()))
    ats = [pl.ds(step * dsts, dsts) for step in range(steps)]
    pick_copies = [
        pltpu.make_async_copy(ref, place, sems.at[steps + i])
        for i, (ref, place) in enumerate(zip(pick_refs, held))
    ]
    ret_copies = [
        pltpu.make_async_copy(
            ret_ref.at[at, pl.ds(ret_ref.shape[1] - ret.shape[1], ret.shape[1])],
            ret.at[at],
            sems.at[step],
        )
        for step, at in enumerate(ats)
    ]
    for copy in pick_copies + ret_copies:
        copy.start()
    for copy in pick_copies:
        copy.wait()
    totals = [None] * len(order)
    for step, at in enumerate(ats):
        ret_copies[step].wait()
        tiles, last = load_tiles(ret[at])
        for source, (which, index) in enumerate(order):
            pick = held[which][index, pl.ds(step * rows, rows), :]
            x = tiles[source].reshape(rows, tiles[source].shape[2]).astype(BF16)
            loss = jnp.dot(last, unit_row(base + source), preferred_element_type=F32).astype(BF16)
            x = jnp.concatenate([x, loss], axis=1)
            out = lax.dot_general(pick, x, over_rows, preferred_element_type=F32)
            totals[source] = out if step == 0 else totals[source] + out
    first = 0
    for source, count in enumerate(parts):
        out = totals[source]
        if source in add_refs:
            out = out + add_refs[source][...].astype(F32)
        part = queries // count
        for i in range(count):
            out_refs[first + i][...] = out[i * part : (i + 1) * part].astype(BF16)
        first += count


def combine(ret, picks, order, parts, width, arrived=(), params=SMALL, base=0):
    queries = picks[0].shape[2]
    shapes = [(queries // count, width + LANES) for count in parts for _ in range(count)]
    added = [a for _, a in arrived]
    steps = 2
    return pl.pallas_call(
        functools.partial(
            combine_kernel,
            order=order,
            picks=len(picks),
            parts=parts,
            added=[i for i, _ in arrived],
            base=base,
            steps=steps,
        ),
        out_shape=[jax.ShapeDtypeStruct(shape, BF16) for shape in shapes],
        in_specs=[IN_HBM] * (1 + len(picks)) + [IN_VMEM] * len(added),
        out_specs=[IN_VMEM] * len(shapes),
        scratch_shapes=[pltpu.VMEM((ret.shape[0], tile_rows_of(sources_of(ret) - base), LANES), BF16)]
        + [pltpu.VMEM(pick.shape, BF16) for pick in picks]
        + [pltpu.SemaphoreType.DMA((steps + len(picks),))],
        compiler_params=params,
        name="combine",
    )(ret, *picks, *added)


def add(a, b):
    return (a.astype(F32) + b.astype(F32)).astype(BF16)


def add_half(a, half, second):
    zero = jnp.zeros_like(half)
    return add(a, jnp.concatenate([zero, half] if second else [half, zero], axis=0))


def overflow(encodings, weights, label_count, matched, positive):
    queries, width = encodings.shape
    top = matched.shape[1]
    per_dst = label_count.shape[0]
    groups, dsts = lax.axis_size("grp"), lax.axis_size("dev")
    receivers = groups * dsts
    labels = weights.shape[0] // per_dst
    flat = matched.reshape(-1)
    item = jnp.arange(queries * top, dtype=jnp.int32)
    same = (flat[:, None] == flat[None, :]) & (item[None, :] < item[:, None])
    second = jnp.any(same, axis=1)
    load = jnp.sum(flat[:, None] // per_dst == jnp.arange(receivers)[None, :], axis=0)
    late = second & (flat % per_dst == per_dst - 1) & (load[flat // per_dst] > SLOTS)
    mine = (flat[:, None] // per_dst == jnp.arange(receivers)[None, :]) & late[:, None]
    there = jnp.any(mine, axis=0)
    which = jnp.argmax(mine, axis=0)
    query = which // top

    def exchange(v):
        v = v.reshape((groups, dsts) + v.shape[1:])
        v = lax.all_to_all(v, "grp", split_axis=0, concat_axis=0, tiled=True)
        v = lax.all_to_all(v, "dev", split_axis=1, concat_axis=1, tiled=True)
        return v.reshape((receivers,) + v.shape[2:])

    rows = exchange(jnp.where(there[:, None], encodings[query], jnp.zeros((), BF16)))
    want = exchange(jnp.where(there, positive.reshape(-1)[which], -1))
    last = weights[(per_dst - 1) * labels :]
    scores = lax.dot_general(rows, last, (((1,), (1,)), ((), ())), preferred_element_type=F32)
    index = jnp.arange(labels, dtype=jnp.int32)[None, :]
    valid = (index < label_count[per_dst - 1]) & (want >= 0)[:, None]
    target = (index == want[:, None]).astype(F32)
    loss = jnp.sum(jnp.where(valid, jax.nn.softplus(scores) - target * scores, 0.0), axis=1)
    grad = jnp.where(valid, jax.nn.sigmoid(scores) - target, 0.0).astype(BF16)
    part = jnp.dot(grad, last, preferred_element_type=F32).astype(BF16)
    weight_part = lax.dot_general(grad, rows, (((0,), (0,)), ((), ())), preferred_element_type=F32)
    part, loss = exchange(part), exchange(loss)
    place = jnp.where(there, query, queries)
    enc_part = jnp.zeros((queries, width), F32).at[place].add(part.astype(F32), mode="drop")
    loss_part = jnp.zeros((queries,), F32).at[place].add(loss, mode="drop")
    return enc_part, loss_part, weight_part


def finish_kernel(mine_ref, lower_ref, upper_ref, grad_ref, loss_ref, grad, loss, sems, *, scale):
    width = grad_ref.shape[1]
    total = mine_ref[...].astype(F32) + lower_ref[...].astype(F32) + upper_ref[...].astype(F32)
    grad[...] = total[:, 0:width].astype(BF16)
    grad_copy = pltpu.make_async_copy(grad, grad_ref, sems.at[0])
    grad_copy.start()
    loss[...] = total[:, width:].T[0:1] * scale
    loss_copy = pltpu.make_async_copy(loss, loss_ref, sems.at[1])
    loss_copy.start()
    grad_copy.wait()
    loss_copy.wait()


def finish(mine, to_lower, to_upper, scale):
    queries, wide = mine.shape
    width = wide - LANES
    return pl.pallas_call(
        functools.partial(finish_kernel, scale=scale),
        out_shape=(
            jax.ShapeDtypeStruct((queries, width), BF16),
            jax.ShapeDtypeStruct((1, queries), F32),
        ),
        in_specs=[IN_VMEM] * 3,
        out_specs=[IN_HBM] * 2,
        scratch_shapes=[
            pltpu.VMEM((queries, width), BF16),
            pltpu.VMEM((1, queries), F32),
            pltpu.SemaphoreType.DMA((2,)),
        ],
        compiler_params=SMALL,
        name="finish",
    )(mine, to_lower, to_upper)


def per_device(encodings, label_weights, label_count, matched, positive):
    queries, width = encodings.shape
    top = matched.shape[1]
    per_dst = label_count.shape[0]
    dsts = lax.axis_size("dev")
    groups = lax.axis_size("grp")
    labels = label_weights.shape[0] // per_dst
    half = queries // 2
    reach = groups // 2
    up_pairs = [(i, (i + 1) % groups) for i in range(groups)]
    down_pairs = [(i, (i - 1) % groups) for i in range(groups)]

    def up(v):
        return lax.ppermute(v, "grp", up_pairs)

    def down(v):
        return lax.ppermute(v, "grp", down_pairs)

    def exchange(v):
        return lax.all_to_all(v, "dev", split_axis=0, concat_axis=0, tiled=True)

    me = lax.axis_index("grp").astype(jnp.int32).reshape(1)
    own = prepare(encodings, matched, positive, per_dst * dsts, per_dst, groups * dsts)
    lower, upper = [own], [own]
    for _ in range(1, reach):
        lower.append(up(lower[-1]))
        upper.append(down(upper[-1]))
    across = (up(lower[-1][:half]), down(upper[-1][half:]))
    chunks = [
        [(own,)],
        [(v[k],) for k in range(1, reach - 1) for v in (lower, upper)],
        [(lower[-1],), (upper[-1],), across],
    ]
    picks, got = [], []
    seen = jnp.zeros((TILE, LANES), F32)
    for sources in chunks:
        send, pick, seen = dispatch(sources, me, seen, dsts, per_dst, top)
        if got:
            send, got[-1] = lax.optimization_barrier((send, got[-1]))
        got.append(exchange(send))
        picks.append(pick)

    block = min(16, dsts)
    mid = list(range(len(chunks[1])))
    part_own, grad_own, _ = score(got[0], label_weights, label_count, block, [[0]])
    part_near, part_mid, grad_mid, _ = score(
        got[1], label_weights, label_count, block, [mid[:2], mid[2:]], part_own
    )
    part_mid, part_near = lax.optimization_barrier((part_mid, part_near))
    part_far, grad_far, over = score(got[2], label_weights, label_count, block, [[0, 1, 2]], part_mid)
    back_far = exchange(part_far)
    weight_grad = weight_gradient(list(zip(got, [grad_own, grad_mid, grad_far])), width, block, per_dst)
    part_near, back_far, weight_grad = lax.optimization_barrier((part_near, back_far, weight_grad))
    back_near = exchange(part_near)

    order = [(0, i) for i in mid[2:]] + [(1, 0), (1, 1), (1, 2)]
    far_most = combine(back_far, picks[2:], [(0, 2)], [2], width, (), PARAMS, len(order) - 1)
    to_lower, to_upper = down(far_most[0]), up(far_most[1])
    back_far, _ = lax.optimization_barrier((back_far, far_most[0]))
    sums = list(combine(back_far, picks[1:], order[:-1], [1] * (len(order) - 1), width, (), PARAMS))
    sums[-2:] = [add_half(sums[-2], to_lower, False), add_half(sums[-1], to_upper, True)]
    to_lower, to_upper = down(sums[-2]), up(sums[-1])
    sums = sums[:-2]
    while sums:
        to_lower, to_upper = down(add(sums[-2], to_lower)), up(add(sums[-1], to_upper))
        sums = sums[:-2]
    order = [(0, 0), (1, 0), (1, 1)]
    arrived = ((1, to_lower), (2, to_upper))
    mine, a, b = combine(back_near, picks[:2], order, [1, 1, 1], width, arrived)
    to_lower, to_upper = down(a), up(b)
    scale = 1.0 / (top * labels)

    def plain(mine, to_lower, to_upper, weight_grad):
        enc_grad, query_loss = finish(mine, to_lower, to_upper, scale)
        return enc_grad, query_loss.reshape(queries), weight_grad

    def with_overflow(mine, to_lower, to_upper, weight_grad):
        enc_part, loss_part, weight_part = overflow(
            encodings, label_weights, label_count, matched, positive
        )
        total = mine.astype(F32) + to_lower.astype(F32) + to_upper.astype(F32)
        enc_grad = (total[:, 0:width] + enc_part).astype(BF16)
        query_loss = (total[:, width] + loss_part) * scale
        return enc_grad, query_loss, weight_grad.at[(per_dst - 1) * labels :].add(weight_part)

    enc_grad, query_loss, weight_grad = lax.cond(
        over[0, LANES - 1] > 0.0, with_overflow, plain, mine, to_lower, to_upper, weight_grad
    )
    return enc_grad, query_loss, weight_grad


def solution(mesh):
    in_specs = (
        P(("grp", "dev"), None),
        P(("grp", "dev"), None),
        P(("grp", "dev")),
        P(("grp", "dev"), None),
        P(("grp", "dev"), None),
    )
    out_specs = (P(("grp", "dev"), None), P(("grp", "dev")), P(("grp", "dev"), None))
    return jax.shard_map(
        per_device, mesh=mesh, in_specs=in_specs, out_specs=out_specs, check_vma=False
    )
```

```python
import functools

import jax
import jax.numpy as jnp
from jax import lax
from jax.experimental import pallas as pl
from jax.experimental.pallas import tpu as pltpu
from jax.sharding import PartitionSpec as P

F32 = jnp.float32
BF16 = jnp.bfloat16
LANES = 128
TILE = 8
META = 16
PARAMS = pltpu.CompilerParams(vmem_limit_bytes=63 * 1024 * 1024)
SMALL = pltpu.CompilerParams(vmem_limit_bytes=28 * 1024 * 1024)
IN_HBM = pl.BlockSpec(memory_space=pltpu.HBM)
IN_VMEM = pl.BlockSpec(memory_space=pltpu.VMEM)

SLOTS = TILE - 1
MOVED = 128


def iota(shape, dim):
    return lax.broadcasted_iota(jnp.int32, shape, dim)


def whole(shape):
    return pl.BlockSpec(shape, lambda i: (0,) * len(shape))


def unit_row(row):
    return (iota((LANES, LANES), 0) == row).astype(BF16)


def unit_column(shape, column):
    return (iota(shape, 1) == column).astype(BF16)


def to_tiles(rows):
    tiles = [rows[:, :, k * LANES : (k + 1) * LANES] for k in range(TILE)]
    under = iota(tiles[0].shape, 1) == SLOTS
    return [jnp.where(under, tiles[SLOTS][:, k : k + 1], tiles[k]) for k in range(SLOTS)]


def store_tiles(ref, at, tiles):
    for k in range(0, len(tiles), 2):
        pair = jnp.concatenate(tiles[k : k + 2], axis=1)
        ref[at, k * TILE : k * TILE + pair.shape[1], :] = pair.astype(BF16)


def load_tiles(held):
    devs, tile_rows, _ = held.shape
    tiles = held.astype(F32).reshape(devs, tile_rows // TILE, TILE, LANES)
    sublane = iota((devs, TILE, LANES), 1)
    rows = []
    for s in range(tile_rows // TILE // SLOTS):
        own = [tiles[:, s * SLOTS + k] for k in range(SLOTS)]
        end = own[0][:, SLOTS : SLOTS + 1]
        for k in range(1, SLOTS):
            end = jnp.where(sublane == k, own[k][:, SLOTS : SLOTS + 1], end)
        rows.append(jnp.concatenate(own + [jnp.broadcast_to(end, own[0].shape)], axis=2))
    return rows, tiles[:, -1].reshape(devs * TILE, LANES).astype(BF16)


def sources_of(x):
    return (x.shape[1] // TILE - 1) // SLOTS


def tile_rows_of(sources):
    return (sources * SLOTS + 1) * TILE


def wanted(last, sources, devs):
    parts = [
        jnp.dot(last, unit_row(s), preferred_element_type=F32).reshape(devs, 1, TILE, LANES)
        for s in range(sources)
    ]
    return jnp.concatenate(parts, axis=1).reshape(devs * sources * TILE, LANES)


def own_cluster(want, per_dst):
    place = iota(want.shape, 0) % per_dst
    return jnp.where(want > MOVED, per_dst - 1, place)


def prepare_kernel(
    enc_ref, matched_ref, positive_ref, out_ref, held, sems, *, in_group, per_dst, receivers
):
    queries = enc_ref.shape[0]
    top = matched_ref.shape[0]
    copies = [
        pltpu.make_async_copy(matched_ref, held.at[0], sems.at[0]),
        pltpu.make_async_copy(positive_ref, held.at[1], sems.at[1]),
        pltpu.make_async_copy(enc_ref, out_ref.at[pl.ds(0, queries)], sems.at[2]),
    ]
    for copy in copies:
        copy.start()
    copies[0].wait()
    copies[1].wait()
    matched = held[0]
    group = matched // in_group
    parts = (group, matched - group * in_group, held[1])
    meta = jnp.concatenate([part.astype(F32) for part in parts], axis=1)
    meta = jnp.concatenate([meta, jnp.zeros((top, out_ref.shape[1] - meta.shape[1]), F32)], axis=1)
    receiver = matched // per_dst
    receivers = iota((receivers, queries), 0)
    load = jnp.zeros(receivers.shape, F32)
    for t in range(top):
        load = load + (receivers == receiver[t : t + 1]).astype(F32)
    load = jnp.max(jnp.sum(load, axis=1, keepdims=True), axis=0, keepdims=True)
    over = jnp.broadcast_to(jnp.where(load > SLOTS, 1.0, 0.0), (META - top, meta.shape[1]))
    meta = jnp.concatenate([meta, over], axis=0)
    out_ref[queries:] = meta.astype(BF16)
    copies[2].wait()


def prepare(encodings, matched, positive, in_group, per_dst, receivers):
    queries, width = encodings.shape
    top = matched.shape[1]
    return pl.pallas_call(
        functools.partial(
            prepare_kernel, in_group=in_group, per_dst=per_dst, receivers=receivers
        ),
        out_shape=jax.ShapeDtypeStruct((queries + META, width), BF16),
        in_specs=[IN_HBM] * 3,
        out_specs=IN_VMEM,
        scratch_shapes=[pltpu.VMEM((2, top, queries), jnp.int32), pltpu.SemaphoreType.DMA((3,))],
        compiler_params=PARAMS,
        name="prepare",
    )(encodings, matched.T, positive.T)


def dispatch_kernel(grp_ref, *refs, parts, top, per_dst, steps):
    x_refs, (seen_ref, send_ref, pick_ref, now_ref, send, picks, sems) = refs[:-7], refs[-7:]
    width = x_refs[0].shape[1]
    queries = pick_ref.shape[2]
    sources = len(parts)
    dsts = send_ref.shape[0] // steps
    rows = dsts * TILE
    me = grp_ref[0].astype(F32)
    row = iota((rows, queries), 0)
    rank = ((row // per_dst) % 2).astype(F32)
    before = (iota((queries, queries), 0) < iota((queries, queries), 1)).astype(BF16)
    blocks, keys, wants, first = [], [], [], 0
    seen = seen_ref[...]
    for count in parts:
        x = jnp.concatenate([r[...] for r in x_refs[first : first + count]], axis=0)
        first += count
        meta = x[queries:].astype(F32)[0:top]
        group, local, slot = [meta[:, i * queries : (i + 1) * queries] for i in range(3)]
        blocks.append(x[0:queries])
        seen = jnp.maximum(seen, x[queries:].astype(F32)[TILE : 2 * TILE, 0:LANES])
        keys.append(jnp.where(group == me, local, -1.0).astype(BF16))
        wants.append((slot + 1.0).astype(BF16))
    now_ref[...] = seen
    ones = jnp.ones((queries, LANES), BF16)
    copies = []
    for step in range(steps):
        cluster = ((row // TILE + step * dsts) * per_dst + row % per_dst).astype(F32).astype(BF16)
        at, at_rows = pl.ds(step * dsts, dsts), pl.ds(step * rows, rows)
        lane = iota((dsts, TILE, LANES), 2)
        sublane = iota((dsts, TILE, LANES), 1)
        last = jnp.where(lane == LANES - 1, jnp.broadcast_to(seen, lane.shape), 0.0)
        tiles = []
        for source in range(sources):
            value = jnp.zeros((rows, queries), BF16)
            for t in range(top):
                same = cluster == keys[source][t : t + 1]
                value = value + jnp.where(same, wants[source][t : t + 1], jnp.zeros((), BF16))
            hit = (value > 0.0).astype(BF16)
            earlier = jnp.dot(hit, before, preferred_element_type=F32)
            value = jnp.where(earlier == rank, value.astype(F32), 0.0)
            want = jnp.dot(value.astype(BF16), ones, preferred_element_type=F32)
            value = value.reshape(dsts, TILE, queries)
            want = want.reshape(dsts, TILE, LANES)
            value_end, want_end = value[:, SLOTS : SLOTS + 1], want[:, SLOTS : SLOTS + 1]
            waiting = want_end > 0.0
            for slot in range(per_dst, SLOTS):
                free = want[:, slot : slot + 1] == 0.0
                here = (sublane == slot) & jnp.broadcast_to(waiting & free, sublane.shape)
                value = jnp.where(here, value_end, value)
                want = jnp.where(here, want_end + MOVED, want)
                waiting = waiting & jnp.logical_not(free)
            value = jnp.where(sublane == SLOTS, 0.0, value)
            want = jnp.where(sublane == SLOTS, 0.0, want)
            pick = (value > 0.0).astype(F32).reshape(rows, queries).astype(BF16)
            picks[source, at_rows, :] = pick
            out = jnp.dot(pick, blocks[source], preferred_element_type=F32)
            tiles.extend(to_tiles(out.reshape(dsts, TILE, width)))
            last = jnp.where(lane == source, want, last)
        store_tiles(send, at, tiles + [last])
        copies.append(pltpu.make_async_copy(send.at[at], send_ref.at[at], sems.at[0, step]))
        copies.append(
            pltpu.make_async_copy(picks.at[:, at_rows], pick_ref.at[:, at_rows], sems.at[1, step])
        )
        copies[-2].start()
        copies[-1].start()
    for copy in copies:
        copy.wait()


def dispatch(sources, grp, seen, dsts, per_dst, top):
    flat = [block for blocks in sources for block in blocks]
    queries = sum(block.shape[0] for block in sources[0]) - META
    send = (dsts, tile_rows_of(len(sources)), LANES)
    pick = (len(sources), dsts * TILE, queries)
    steps = 2
    return pl.pallas_call(
        functools.partial(
            dispatch_kernel,
            parts=[len(blocks) for blocks in sources],
            top=top,
            per_dst=per_dst,
            steps=steps,
        ),
        out_shape=(
            jax.ShapeDtypeStruct(send, BF16),
            jax.ShapeDtypeStruct(pick, BF16),
            jax.ShapeDtypeStruct((TILE, LANES), F32),
        ),
        in_specs=[pl.BlockSpec(memory_space=pltpu.SMEM)] + [IN_VMEM] * (len(flat) + 1),
        out_specs=[IN_HBM, IN_HBM, IN_VMEM],
        scratch_shapes=[
            pltpu.VMEM(send, BF16),
            pltpu.VMEM(pick, BF16),
            pltpu.SemaphoreType.DMA((2, steps)),
        ],
        compiler_params=SMALL,
        name="dispatch",
    )(grp, *flat, seen)


def own_columns(grad, own, per_dst):
    return jnp.concatenate([jnp.where(own == cl, grad, 0.0) for cl in range(per_dst)], axis=1).astype(BF16)


def score_kernel(count_ref, x_ref, w_ref, *refs, per_dst, carried, outs):
    carry_ref, ret_refs = refs[0], refs[1 if carried else 0 : -2]
    grad_ref, over_ref = refs[-2:]
    devs = x_ref.shape[0]
    all_labels, width = w_ref.shape
    labels = all_labels // per_dst
    tiles, last = load_tiles(x_ref[...])
    sources = len(tiles)
    rows = devs * sources * TILE
    x = jnp.concatenate([t.reshape(devs, 1, TILE, width) for t in tiles], axis=1)
    x = x.reshape(rows, width).astype(BF16)
    want = wanted(last, sources, devs)
    scores = lax.dot_general(
        x, w_ref[...], (((1,), (1,)), ((), ())), preferred_element_type=F32
    )
    own = own_cluster(want, per_dst)
    want = jnp.where(want > MOVED, want - MOVED, want)
    label = iota((rows, labels), 1)
    s = scores[:, 0:labels]
    count = jnp.full((rows, labels), count_ref[0], jnp.int32)
    for cl in range(1, per_dst):
        s = jnp.where(own == cl, scores[:, cl * labels : (cl + 1) * labels], s)
        count = jnp.where(own == cl, count_ref[cl], count)
    valid = (label < count) & (want > 0.0)
    target = (label.astype(F32) + 1.0) == want
    small = jnp.exp(-jnp.abs(s))
    soft = jnp.maximum(s, 0.0) + jnp.log(1.0 + small)
    term = jnp.where(valid, soft - jnp.where(target, s, 0.0), 0.0)
    loss = jnp.sum(term, axis=1, keepdims=True).reshape(devs, sources, TILE, 1)
    sig = jnp.where(s >= 0.0, 1.0, small) / (1.0 + small)
    grad = jnp.where(valid, sig - jnp.where(target, 1.0, 0.0), 0.0)
    grad_ref[...] = grad.astype(BF16)
    part = jnp.dot(own_columns(grad, own, per_dst), w_ref[...], preferred_element_type=F32)
    part = part.reshape(devs, sources, TILE, width)
    lane = iota((devs, TILE, LANES), 2)
    for i, (ret_ref, members) in enumerate(zip(ret_refs, outs)):
        before = carried if i == 0 else 0
        back, end = [], jnp.zeros((devs, TILE, LANES), F32)
        if before:
            carry = carry_ref[...].astype(F32).reshape(devs, before * SLOTS + 1, TILE, LANES)
            back = [carry[:, k] for k in range(before * SLOTS)]
            end = carry[:, before * SLOTS]
        for j, source in enumerate(members):
            back.extend(to_tiles(part[:, source]))
            end = jnp.where(lane == before + j, loss[:, source], end)
        store_tiles(ret_ref, slice(None), back + [end])
    over = jnp.max(last.astype(F32).reshape(devs, TILE, LANES), axis=0)

    @pl.when(pl.program_id(0) == 0)
    def _():
        over_ref[...] = over

    @pl.when(pl.program_id(0) > 0)
    def _():
        over_ref[...] = jnp.maximum(over_ref[...], over)


def score(x, weights, count, block, outs, carry=None):
    devs, tile_rows, _ = x.shape
    per_dst = count.shape[0]
    all_labels, width = weights.shape
    labels = all_labels // per_dst
    slots = sources_of(x) * TILE
    carried = sources_of(carry) if carry is not None else 0
    sizes = [len(members) + (carried if i == 0 else 0) for i, members in enumerate(outs)]
    ret_rows = [tile_rows_of(size) for size in sizes]

    def by_dev(rows):
        return pl.BlockSpec((block, rows, LANES), lambda i: (i, 0, 0))

    return pl.pallas_call(
        functools.partial(score_kernel, per_dst=per_dst, carried=carried, outs=outs),
        grid=(devs // block,),
        out_shape=[jax.ShapeDtypeStruct((devs, r, LANES), BF16) for r in ret_rows]
        + [
            jax.ShapeDtypeStruct((devs * slots, labels), BF16),
            jax.ShapeDtypeStruct((TILE, LANES), F32),
        ],
        in_specs=[
            pl.BlockSpec(memory_space=pltpu.SMEM),
            by_dev(tile_rows),
            whole((all_labels, width)),
        ]
        + ([by_dev(carry.shape[1])] if carried else []),
        out_specs=[by_dev(r) for r in ret_rows]
        + [pl.BlockSpec((block * slots, labels), lambda i: (i, 0)), whole((TILE, LANES))],
        compiler_params=PARAMS,
        cost_estimate=pl.CostEstimate(
            flops=4 * devs * slots * all_labels * width,
            bytes_accessed=4 * devs * slots * (width + labels) + 2 * all_labels * width,
            transcendentals=0,
        ),
        name="score",
    )(count, x, weights, *([carry] if carried else []))


def weight_kernel(*refs, per_dst):
    out_ref = refs[-1]
    width = out_ref.shape[1]
    total = None
    for x_ref, grad_ref in zip(refs[0:-1:2], refs[1:-1:2]):
        tiles, last = load_tiles(x_ref[...])
        devs = x_ref.shape[0]
        own = own_cluster(wanted(last, len(tiles), devs), per_dst)
        x = jnp.concatenate([t.reshape(devs, 1, TILE, width) for t in tiles], axis=1)
        x = x.reshape(devs * len(tiles) * TILE, width).astype(BF16)
        grad = own_columns(grad_ref[...].astype(F32), own, per_dst)
        part = lax.dot_general(
            grad, x, (((0,), (0,)), ((), ())), preferred_element_type=F32
        )
        total = part if total is None else total + part

    @pl.when(pl.program_id(0) == 0)
    def _():
        out_ref[...] = total

    @pl.when(pl.program_id(0) > 0)
    def _():
        out_ref[...] += total


def weight_gradient(chunks, width, block, per_dst):
    labels = chunks[0][1].shape[1]
    all_labels = labels * per_dst
    devs = chunks[0][0].shape[0]
    rows = sum(grad.shape[0] for _, grad in chunks)
    flat = [a for chunk in chunks for a in chunk]
    specs = []
    for x, grad in chunks:
        specs.append(pl.BlockSpec((block,) + x.shape[1:], lambda i: (i, 0, 0)))
        specs.append(pl.BlockSpec((grad.shape[0] * block // devs, labels), lambda i: (i, 0)))
    return pl.pallas_call(
        functools.partial(weight_kernel, per_dst=per_dst),
        grid=(devs // block,),
        out_shape=jax.ShapeDtypeStruct((all_labels, width), F32),
        in_specs=specs,
        out_specs=whole((all_labels, width)),
        compiler_params=PARAMS,
        cost_estimate=pl.CostEstimate(
            flops=2 * rows * all_labels * width,
            bytes_accessed=2 * rows * (width + all_labels) + 4 * all_labels * width,
            transcendentals=0,
        ),
        name="weight_gradient",
    )(*flat)


def combine_kernel(ret_ref, *refs, order, picks, parts, added, base, steps):
    pick_refs, refs = refs[:picks], refs[picks:]
    add_refs, refs = dict(zip(added, refs[: len(added)])), refs[len(added) :]
    out_refs, ret = refs[: sum(parts)], refs[sum(parts)]
    held, sems = refs[sum(parts) + 1 : -1], refs[-1]
    dsts = ret_ref.shape[0] // steps
    queries = held[0].shape[2]
    rows = dsts * TILE
    over_rows = (((0,), (0,)), ((), ()))
    ats = [pl.ds(step * dsts, dsts) for step in range(steps)]
    pick_copies = [
        pltpu.make_async_copy(ref, place, sems.at[steps + i])
        for i, (ref, place) in enumerate(zip(pick_refs, held))
    ]
    ret_copies = [
        pltpu.make_async_copy(
            ret_ref.at[at, pl.ds(ret_ref.shape[1] - ret.shape[1], ret.shape[1])],
            ret.at[at],
            sems.at[step],
        )
        for step, at in enumerate(ats)
    ]
    for copy in pick_copies + ret_copies:
        copy.start()
    for copy in pick_copies:
        copy.wait()
    totals = [None] * len(order)
    for step, at in enumerate(ats):
        ret_copies[step].wait()
        tiles, last = load_tiles(ret[at])
        for source, (which, index) in enumerate(order):
            pick = held[which][index, pl.ds(step * rows, rows), :]
            x = tiles[source].reshape(rows, tiles[source].shape[2]).astype(BF16)
            loss = jnp.dot(last, unit_row(base + source), preferred_element_type=F32).astype(BF16)
            x = jnp.concatenate([x, loss], axis=1)
            out = lax.dot_general(pick, x, over_rows, preferred_element_type=F32)
            totals[source] = out if step == 0 else totals[source] + out
    first = 0
    for source, count in enumerate(parts):
        out = totals[source]
        if source in add_refs:
            out = out + add_refs[source][...].astype(F32)
        part = queries // count
        for i in range(count):
            out_refs[first + i][...] = out[i * part : (i + 1) * part].astype(BF16)
        first += count


def combine(ret, picks, order, parts, width, arrived=(), params=SMALL, base=0):
    queries = picks[0].shape[2]
    shapes = [(queries // count, width + LANES) for count in parts for _ in range(count)]
    added = [a for _, a in arrived]
    steps = 2
    return pl.pallas_call(
        functools.partial(
            combine_kernel,
            order=order,
            picks=len(picks),
            parts=parts,
            added=[i for i, _ in arrived],
            base=base,
            steps=steps,
        ),
        out_shape=[jax.ShapeDtypeStruct(shape, BF16) for shape in shapes],
        in_specs=[IN_HBM] * (1 + len(picks)) + [IN_VMEM] * len(added),
        out_specs=[IN_VMEM] * len(shapes),
        scratch_shapes=[pltpu.VMEM((ret.shape[0], tile_rows_of(sources_of(ret) - base), LANES), BF16)]
        + [pltpu.VMEM(pick.shape, BF16) for pick in picks]
        + [pltpu.SemaphoreType.DMA((steps + len(picks),))],
        compiler_params=params,
        name="combine",
    )(ret, *picks, *added)


def add(a, b):
    return (a.astype(F32) + b.astype(F32)).astype(BF16)


def add_half(a, half, second):
    zero = jnp.zeros_like(half)
    return add(a, jnp.concatenate([zero, half] if second else [half, zero], axis=0))


def overflow(encodings, weights, label_count, matched, positive):
    queries, width = encodings.shape
    top = matched.shape[1]
    per_dst = label_count.shape[0]
    groups, dsts = lax.axis_size("grp"), lax.axis_size("dev")
    receivers = groups * dsts
    labels = weights.shape[0] // per_dst
    flat = matched.reshape(-1)
    item = jnp.arange(queries * top, dtype=jnp.int32)
    same = (flat[:, None] == flat[None, :]) & (item[None, :] < item[:, None])
    second = jnp.any(same, axis=1, keepdims=True)
    to = flat[:, None] // per_dst == jnp.arange(receivers)[None, :]
    full = jnp.sum(to, axis=0, keepdims=True) > SLOTS
    late = to & full & second & (flat % per_dst == per_dst - 1)[:, None]
    value = jnp.where(late, positive.reshape(-1, 1) + 1, 0).reshape(queries, top, receivers)
    value = jnp.sum(value, axis=1).astype(BF16)
    pick = (value > 0).astype(BF16)

    def exchange(rows, extra):
        extra = jnp.broadcast_to(extra.astype(BF16), (receivers, LANES))
        v = jnp.concatenate([rows, extra], axis=1)
        v = lax.all_to_all(v, ("grp", "dev"), split_axis=0, concat_axis=0, tiled=True)
        return v[:, 0:width], v[:, width : width + 1]

    turned = (((0,), (0,)), ((), ()))
    rows = lax.dot_general(pick, encodings, turned, preferred_element_type=F32).astype(BF16)
    rows, want = exchange(rows, jnp.sum(value.astype(F32), axis=0)[:, None])
    last = weights[(per_dst - 1) * labels :]
    scores = lax.dot_general(rows, last, (((1,), (1,)), ((), ())), preferred_element_type=F32)
    index = jnp.arange(labels, dtype=jnp.int32)[None, :]
    valid = (index < label_count[per_dst - 1]) & (want > 0)
    target = ((index + 1).astype(F32) == want.astype(F32)).astype(F32)
    soft = jnp.maximum(scores, 0.0) + jnp.log(1.0 + jnp.exp(-jnp.abs(scores)))
    loss = jnp.sum(jnp.where(valid, soft - target * scores, 0.0), axis=1, keepdims=True)
    grad = jnp.where(valid, jax.nn.sigmoid(scores) - target, 0.0).astype(BF16)
    part = jnp.dot(grad, last, preferred_element_type=F32).astype(BF16)
    weight_part = lax.dot_general(grad, rows, turned, preferred_element_type=F32)
    part, loss = exchange(part, loss)
    enc_part = jnp.dot(pick, part, preferred_element_type=F32)
    loss_part = jnp.dot(pick, loss, preferred_element_type=F32)[:, 0]
    return enc_part, loss_part, weight_part


def finish_kernel(mine_ref, lower_ref, upper_ref, grad_ref, loss_ref, grad, loss, sems, *, scale):
    width = grad_ref.shape[1]
    total = mine_ref[...].astype(F32) + lower_ref[...].astype(F32) + upper_ref[...].astype(F32)
    grad[...] = total[:, 0:width].astype(BF16)
    grad_copy = pltpu.make_async_copy(grad, grad_ref, sems.at[0])
    grad_copy.start()
    loss[...] = total[:, width:].T[0:1] * scale
    loss_copy = pltpu.make_async_copy(loss, loss_ref, sems.at[1])
    loss_copy.start()
    grad_copy.wait()
    loss_copy.wait()


def finish(mine, to_lower, to_upper, scale):
    queries, wide = mine.shape
    width = wide - LANES
    return pl.pallas_call(
        functools.partial(finish_kernel, scale=scale),
        out_shape=(
            jax.ShapeDtypeStruct((queries, width), BF16),
            jax.ShapeDtypeStruct((1, queries), F32),
        ),
        in_specs=[IN_VMEM] * 3,
        out_specs=[IN_HBM] * 2,
        scratch_shapes=[
            pltpu.VMEM((queries, width), BF16),
            pltpu.VMEM((1, queries), F32),
            pltpu.SemaphoreType.DMA((2,)),
        ],
        compiler_params=SMALL,
        name="finish",
    )(mine, to_lower, to_upper)


def per_device(encodings, label_weights, label_count, matched, positive):
    queries, width = encodings.shape
    top = matched.shape[1]
    per_dst = label_count.shape[0]
    dsts = lax.axis_size("dev")
    groups = lax.axis_size("grp")
    labels = label_weights.shape[0] // per_dst
    half = queries // 2
    reach = groups // 2
    up_pairs = [(i, (i + 1) % groups) for i in range(groups)]
    down_pairs = [(i, (i - 1) % groups) for i in range(groups)]

    def up(v):
        return lax.ppermute(v, "grp", up_pairs)

    def down(v):
        return lax.ppermute(v, "grp", down_pairs)

    def exchange(v):
        return lax.all_to_all(v, "dev", split_axis=0, concat_axis=0, tiled=True)

    me = lax.axis_index("grp").astype(jnp.int32).reshape(1)
    own = prepare(encodings, matched, positive, per_dst * dsts, per_dst, groups * dsts)
    lower, upper = [own], [own]
    for _ in range(1, reach):
        lower.append(up(lower[-1]))
        upper.append(down(upper[-1]))
    across = (up(lower[-1][:half]), down(upper[-1][half:]))
    chunks = [
        [(own,)],
        [(v[k],) for k in range(1, reach - 1) for v in (lower, upper)],
        [(lower[-1],), (upper[-1],), across],
    ]
    picks, got = [], []
    seen = jnp.zeros((TILE, LANES), F32)
    for sources in chunks:
        send, pick, seen = dispatch(sources, me, seen, dsts, per_dst, top)
        if got:
            send, got[-1] = lax.optimization_barrier((send, got[-1]))
        got.append(exchange(send))
        picks.append(pick)

    block = min(16, dsts)
    mid = list(range(len(chunks[1])))
    part_own, grad_own, _ = score(got[0], label_weights, label_count, block, [[0]])
    part_near, part_mid, grad_mid, _ = score(
        got[1], label_weights, label_count, block, [mid[:2], mid[2:]], part_own
    )
    part_mid, part_near = lax.optimization_barrier((part_mid, part_near))
    part_far, grad_far, over = score(got[2], label_weights, label_count, block, [[0, 1, 2]], part_mid)
    back_far = exchange(part_far)
    weight_grad = weight_gradient(list(zip(got, [grad_own, grad_mid, grad_far])), width, block, per_dst)
    part_near, back_far, weight_grad = lax.optimization_barrier((part_near, back_far, weight_grad))
    back_near = exchange(part_near)

    order = [(0, i) for i in mid[2:]] + [(1, 0), (1, 1), (1, 2)]
    far_most = combine(back_far, picks[2:], [(0, 2)], [2], width, (), PARAMS, len(order) - 1)
    to_lower, to_upper = down(far_most[0]), up(far_most[1])
    back_far, _ = lax.optimization_barrier((back_far, far_most[0]))
    sums = list(combine(back_far, picks[1:], order[:-1], [1] * (len(order) - 1), width, (), PARAMS))
    sums[-2:] = [add_half(sums[-2], to_lower, False), add_half(sums[-1], to_upper, True)]
    to_lower, to_upper = down(sums[-2]), up(sums[-1])
    sums = sums[:-2]
    while sums:
        to_lower, to_upper = down(add(sums[-2], to_lower)), up(add(sums[-1], to_upper))
        sums = sums[:-2]
    order = [(0, 0), (1, 0), (1, 1)]
    arrived = ((1, to_lower), (2, to_upper))
    mine, a, b = combine(back_near, picks[:2], order, [1, 1, 1], width, arrived)
    to_lower, to_upper = down(a), up(b)
    scale = 1.0 / (top * labels)

    def plain(mine, to_lower, to_upper, weight_grad):
        enc_grad, query_loss = finish(mine, to_lower, to_upper, scale)
        return enc_grad, query_loss.reshape(queries), weight_grad

    def with_overflow(mine, to_lower, to_upper, weight_grad):
        enc_part, loss_part, weight_part = overflow(
            encodings, label_weights, label_count, matched, positive
        )
        total = mine.astype(F32) + to_lower.astype(F32) + to_upper.astype(F32)
        enc_grad = (total[:, 0:width] + enc_part).astype(BF16)
        query_loss = (total[:, width] + loss_part) * scale
        return enc_grad, query_loss, weight_grad.at[(per_dst - 1) * labels :].add(weight_part)

    enc_grad, query_loss, weight_grad = lax.cond(
        over[0, LANES - 1] > 0.0, with_overflow, plain, mine, to_lower, to_upper, weight_grad
    )
    return enc_grad, query_loss, weight_grad


def solution(mesh):
    in_specs = (
        P(("grp", "dev"), None),
        P(("grp", "dev"), None),
        P(("grp", "dev")),
        P(("grp", "dev"), None),
        P(("grp", "dev"), None),
    )
    out_specs = (P(("grp", "dev"), None), P(("grp", "dev")), P(("grp", "dev"), None))
    return jax.shard_map(
        per_device, mesh=mesh, in_specs=in_specs, out_specs=out_specs, check_vma=False
    )
```

```python
import functools

import jax
import jax.numpy as jnp
from jax import lax
from jax.experimental import pallas as pl
from jax.experimental.pallas import tpu as pltpu
from jax.sharding import PartitionSpec as P

F32 = jnp.float32
BF16 = jnp.bfloat16
LANES = 128
TILE = 8
META = 16
PARAMS = pltpu.CompilerParams(vmem_limit_bytes=63 * 1024 * 1024)
SMALL = pltpu.CompilerParams(vmem_limit_bytes=28 * 1024 * 1024)
IN_HBM = pl.BlockSpec(memory_space=pltpu.HBM)
IN_VMEM = pl.BlockSpec(memory_space=pltpu.VMEM)

SLOTS = TILE - 1
MOVED = 128


def iota(shape, dim):
    return lax.broadcasted_iota(jnp.int32, shape, dim)


def whole(shape):
    return pl.BlockSpec(shape, lambda i: (0,) * len(shape))


def unit_row(row):
    return (iota((LANES, LANES), 0) == row).astype(BF16)


def unit_column(shape, column):
    return (iota(shape, 1) == column).astype(BF16)


def to_tiles(rows):
    tiles = [rows[:, :, k * LANES : (k + 1) * LANES] for k in range(TILE)]
    under = iota(tiles[0].shape, 1) == SLOTS
    return [jnp.where(under, tiles[SLOTS][:, k : k + 1], tiles[k]) for k in range(SLOTS)]


def store_tiles(ref, at, tiles):
    for k in range(0, len(tiles), 2):
        pair = jnp.concatenate(tiles[k : k + 2], axis=1)
        ref[at, k * TILE : k * TILE + pair.shape[1], :] = pair.astype(BF16)


def load_tiles(held):
    devs, tile_rows, _ = held.shape
    tiles = held.astype(F32).reshape(devs, tile_rows // TILE, TILE, LANES)
    sublane = iota((devs, TILE, LANES), 1)
    rows = []
    for s in range(tile_rows // TILE // SLOTS):
        own = [tiles[:, s * SLOTS + k] for k in range(SLOTS)]
        end = own[0][:, SLOTS : SLOTS + 1]
        for k in range(1, SLOTS):
            end = jnp.where(sublane == k, own[k][:, SLOTS : SLOTS + 1], end)
        rows.append(jnp.concatenate(own + [jnp.broadcast_to(end, own[0].shape)], axis=2))
    return rows, tiles[:, -1].reshape(devs * TILE, LANES).astype(BF16)


def sources_of(x):
    return (x.shape[1] // TILE - 1) // SLOTS


def tile_rows_of(sources):
    return (sources * SLOTS + 1) * TILE


def wanted(last, sources, devs):
    parts = [
        jnp.dot(last, unit_row(s), preferred_element_type=F32).reshape(devs, 1, TILE, LANES)
        for s in range(sources)
    ]
    return jnp.concatenate(parts, axis=1).reshape(devs * sources * TILE, LANES)


def own_cluster(want, per_dst):
    place = iota(want.shape, 0) % per_dst
    return jnp.where(want > MOVED, per_dst - 1, place)


def prepare_kernel(
    enc_ref, matched_ref, positive_ref, out_ref, held, sems, *, in_group, per_dst, receivers
):
    queries = enc_ref.shape[0]
    top = matched_ref.shape[0]
    copies = [
        pltpu.make_async_copy(matched_ref, held.at[0], sems.at[0]),
        pltpu.make_async_copy(positive_ref, held.at[1], sems.at[1]),
        pltpu.make_async_copy(enc_ref, out_ref.at[pl.ds(0, queries)], sems.at[2]),
    ]
    for copy in copies:
        copy.start()
    copies[0].wait()
    copies[1].wait()
    matched = held[0]
    group = matched // in_group
    parts = (group, matched - group * in_group, held[1])
    meta = jnp.concatenate([part.astype(F32) for part in parts], axis=1)
    meta = jnp.concatenate([meta, jnp.zeros((top, out_ref.shape[1] - meta.shape[1]), F32)], axis=1)
    receiver = matched // per_dst
    receivers = iota((receivers, queries), 0)
    load = jnp.zeros(receivers.shape, F32)
    for t in range(top):
        load = load + (receivers == receiver[t : t + 1]).astype(F32)
    load = jnp.max(jnp.sum(load, axis=1, keepdims=True), axis=0, keepdims=True)
    over = jnp.broadcast_to(jnp.where(load > SLOTS, 1.0, 0.0), (META - top, meta.shape[1]))
    meta = jnp.concatenate([meta, over], axis=0)
    out_ref[queries:] = meta.astype(BF16)
    copies[2].wait()


def prepare(encodings, matched, positive, in_group, per_dst, receivers):
    queries, width = encodings.shape
    top = matched.shape[1]
    return pl.pallas_call(
        functools.partial(
            prepare_kernel, in_group=in_group, per_dst=per_dst, receivers=receivers
        ),
        out_shape=jax.ShapeDtypeStruct((queries + META, width), BF16),
        in_specs=[IN_HBM] * 3,
        out_specs=IN_VMEM,
        scratch_shapes=[pltpu.VMEM((2, top, queries), jnp.int32), pltpu.SemaphoreType.DMA((3,))],
        compiler_params=PARAMS,
        name="prepare",
    )(encodings, matched.T, positive.T)


def dispatch_kernel(grp_ref, *refs, parts, top, per_dst, steps):
    x_refs, (seen_ref, send_ref, pick_ref, now_ref, send, picks, sems) = refs[:-7], refs[-7:]
    width = x_refs[0].shape[1]
    queries = pick_ref.shape[2]
    sources = len(parts)
    dsts = send_ref.shape[0] // steps
    rows = dsts * TILE
    me = grp_ref[0].astype(F32)
    row = iota((rows, queries), 0)
    rank = ((row // per_dst) % 2).astype(F32)
    before = (iota((queries, queries), 0) < iota((queries, queries), 1)).astype(BF16)
    blocks, keys, wants, first = [], [], [], 0
    seen = seen_ref[...]
    for count in parts:
        x = jnp.concatenate([r[...] for r in x_refs[first : first + count]], axis=0)
        first += count
        meta = x[queries:].astype(F32)[0:top]
        group, local, slot = [meta[:, i * queries : (i + 1) * queries] for i in range(3)]
        blocks.append(x[0:queries])
        seen = jnp.maximum(seen, x[queries:].astype(F32)[TILE : 2 * TILE, 0:LANES])
        keys.append(jnp.where(group == me, local, -1.0).astype(BF16))
        wants.append((slot + 1.0).astype(BF16))
    now_ref[...] = seen
    ones = jnp.ones((queries, LANES), BF16)
    copies = []
    for step in range(steps):
        cluster = ((row // TILE + step * dsts) * per_dst + row % per_dst).astype(F32).astype(BF16)
        at, at_rows = pl.ds(step * dsts, dsts), pl.ds(step * rows, rows)
        lane = iota((dsts, TILE, LANES), 2)
        sublane = iota((dsts, TILE, LANES), 1)
        last = jnp.where(lane == LANES - 1, jnp.broadcast_to(seen, lane.shape), 0.0)
        tiles = []
        for source in range(sources):
            value = jnp.zeros((rows, queries), BF16)
            for t in range(top):
                same = cluster == keys[source][t : t + 1]
                value = value + jnp.where(same, wants[source][t : t + 1], jnp.zeros((), BF16))
            hit = (value > 0.0).astype(BF16)
            earlier = jnp.dot(hit, before, preferred_element_type=F32)
            value = jnp.where(earlier == rank, value.astype(F32), 0.0)
            want = jnp.dot(value.astype(BF16), ones, preferred_element_type=F32)
            value = value.reshape(dsts, TILE, queries)
            want = want.reshape(dsts, TILE, LANES)
            value_end, want_end = value[:, SLOTS : SLOTS + 1], want[:, SLOTS : SLOTS + 1]
            waiting = want_end > 0.0
            for slot in range(per_dst, SLOTS):
                free = want[:, slot : slot + 1] == 0.0
                here = (sublane == slot) & jnp.broadcast_to(waiting & free, sublane.shape)
                value = jnp.where(here, value_end, value)
                want = jnp.where(here, want_end + MOVED, want)
                waiting = waiting & jnp.logical_not(free)
            value = jnp.where(sublane == SLOTS, 0.0, value)
            want = jnp.where(sublane == SLOTS, 0.0, want)
            pick = (value > 0.0).astype(F32).reshape(rows, queries).astype(BF16)
            picks[source, at_rows, :] = pick
            out = jnp.dot(pick, blocks[source], preferred_element_type=F32)
            tiles.extend(to_tiles(out.reshape(dsts, TILE, width)))
            last = jnp.where(lane == source, want, last)
        store_tiles(send, at, tiles + [last])
        copies.append(pltpu.make_async_copy(send.at[at], send_ref.at[at], sems.at[0, step]))
        copies.append(
            pltpu.make_async_copy(picks.at[:, at_rows], pick_ref.at[:, at_rows], sems.at[1, step])
        )
        copies[-2].start()
        copies[-1].start()
    for copy in copies:
        copy.wait()


def dispatch(sources, grp, seen, dsts, per_dst, top):
    flat = [block for blocks in sources for block in blocks]
    queries = sum(block.shape[0] for block in sources[0]) - META
    send = (dsts, tile_rows_of(len(sources)), LANES)
    pick = (len(sources), dsts * TILE, queries)
    steps = 2
    return pl.pallas_call(
        functools.partial(
            dispatch_kernel,
            parts=[len(blocks) for blocks in sources],
            top=top,
            per_dst=per_dst,
            steps=steps,
        ),
        out_shape=(
            jax.ShapeDtypeStruct(send, BF16),
            jax.ShapeDtypeStruct(pick, BF16),
            jax.ShapeDtypeStruct((TILE, LANES), F32),
        ),
        in_specs=[pl.BlockSpec(memory_space=pltpu.SMEM)] + [IN_VMEM] * (len(flat) + 1),
        out_specs=[IN_HBM, IN_HBM, IN_VMEM],
        scratch_shapes=[
            pltpu.VMEM(send, BF16),
            pltpu.VMEM(pick, BF16),
            pltpu.SemaphoreType.DMA((2, steps)),
        ],
        compiler_params=SMALL,
        name="dispatch",
    )(grp, *flat, seen)


def own_columns(grad, own, per_dst):
    return jnp.concatenate([jnp.where(own == cl, grad, 0.0) for cl in range(per_dst)], axis=1).astype(BF16)


def score_kernel(count_ref, x_ref, w_ref, *refs, per_dst, carried, outs):
    carry_ref, ret_refs = refs[0], refs[1 if carried else 0 : -2]
    grad_ref, over_ref = refs[-2:]
    devs = x_ref.shape[0]
    all_labels, width = w_ref.shape
    labels = all_labels // per_dst
    tiles, last = load_tiles(x_ref[...])
    sources = len(tiles)
    rows = devs * sources * TILE
    x = jnp.concatenate([t.reshape(devs, 1, TILE, width) for t in tiles], axis=1)
    x = x.reshape(rows, width).astype(BF16)
    want = wanted(last, sources, devs)
    scores = lax.dot_general(
        x, w_ref[...], (((1,), (1,)), ((), ())), preferred_element_type=F32
    )
    own = own_cluster(want, per_dst)
    want = jnp.where(want > MOVED, want - MOVED, want)
    label = iota((rows, labels), 1)
    s = scores[:, 0:labels]
    count = jnp.full((rows, labels), count_ref[0], jnp.int32)
    for cl in range(1, per_dst):
        s = jnp.where(own == cl, scores[:, cl * labels : (cl + 1) * labels], s)
        count = jnp.where(own == cl, count_ref[cl], count)
    valid = (label < count) & (want > 0.0)
    target = (label.astype(F32) + 1.0) == want
    small = jnp.exp(-jnp.abs(s))
    soft = jnp.maximum(s, 0.0) + jnp.log(1.0 + small)
    term = jnp.where(valid, soft - jnp.where(target, s, 0.0), 0.0)
    loss = jnp.sum(term, axis=1, keepdims=True).reshape(devs, sources, TILE, 1)
    sig = jnp.where(s >= 0.0, 1.0, small) / (1.0 + small)
    grad = jnp.where(valid, sig - jnp.where(target, 1.0, 0.0), 0.0)
    grad_ref[...] = grad.astype(BF16)
    part = jnp.dot(own_columns(grad, own, per_dst), w_ref[...], preferred_element_type=F32)
    part = part.reshape(devs, sources, TILE, width)
    lane = iota((devs, TILE, LANES), 2)
    for i, (ret_ref, members) in enumerate(zip(ret_refs, outs)):
        before = carried if i == 0 else 0
        back, end = [], jnp.zeros((devs, TILE, LANES), F32)
        if before:
            carry = carry_ref[...].astype(F32).reshape(devs, before * SLOTS + 1, TILE, LANES)
            back = [carry[:, k] for k in range(before * SLOTS)]
            end = carry[:, before * SLOTS]
        for j, source in enumerate(members):
            back.extend(to_tiles(part[:, source]))
            end = jnp.where(lane == before + j, loss[:, source], end)
        store_tiles(ret_ref, slice(None), back + [end])
    over = jnp.max(last.astype(F32).reshape(devs, TILE, LANES), axis=0)

    @pl.when(pl.program_id(0) == 0)
    def _():
        over_ref[...] = over

    @pl.when(pl.program_id(0) > 0)
    def _():
        over_ref[...] = jnp.maximum(over_ref[...], over)


def score(x, weights, count, block, outs, carry=None):
    devs, tile_rows, _ = x.shape
    per_dst = count.shape[0]
    all_labels, width = weights.shape
    labels = all_labels // per_dst
    slots = sources_of(x) * TILE
    carried = sources_of(carry) if carry is not None else 0
    sizes = [len(members) + (carried if i == 0 else 0) for i, members in enumerate(outs)]
    ret_rows = [tile_rows_of(size) for size in sizes]

    def by_dev(rows):
        return pl.BlockSpec((block, rows, LANES), lambda i: (i, 0, 0))

    return pl.pallas_call(
        functools.partial(score_kernel, per_dst=per_dst, carried=carried, outs=outs),
        grid=(devs // block,),
        out_shape=[jax.ShapeDtypeStruct((devs, r, LANES), BF16) for r in ret_rows]
        + [
            jax.ShapeDtypeStruct((devs * slots, labels), BF16),
            jax.ShapeDtypeStruct((TILE, LANES), F32),
        ],
        in_specs=[
            pl.BlockSpec(memory_space=pltpu.SMEM),
            by_dev(tile_rows),
            whole((all_labels, width)),
        ]
        + ([by_dev(carry.shape[1])] if carried else []),
        out_specs=[by_dev(r) for r in ret_rows]
        + [pl.BlockSpec((block * slots, labels), lambda i: (i, 0)), whole((TILE, LANES))],
        compiler_params=PARAMS,
        cost_estimate=pl.CostEstimate(
            flops=4 * devs * slots * all_labels * width,
            bytes_accessed=4 * devs * slots * (width + labels) + 2 * all_labels * width,
            transcendentals=0,
        ),
        name="score",
    )(count, x, weights, *([carry] if carried else []))


def weight_kernel(*refs, per_dst):
    out_ref = refs[-1]
    width = out_ref.shape[1]
    total = None
    for x_ref, grad_ref in zip(refs[0:-1:2], refs[1:-1:2]):
        tiles, last = load_tiles(x_ref[...])
        devs = x_ref.shape[0]
        own = own_cluster(wanted(last, len(tiles), devs), per_dst)
        x = jnp.concatenate([t.reshape(devs, 1, TILE, width) for t in tiles], axis=1)
        x = x.reshape(devs * len(tiles) * TILE, width).astype(BF16)
        grad = own_columns(grad_ref[...].astype(F32), own, per_dst)
        part = lax.dot_general(
            grad, x, (((0,), (0,)), ((), ())), preferred_element_type=F32
        )
        total = part if total is None else total + part

    @pl.when(pl.program_id(0) == 0)
    def _():
        out_ref[...] = total

    @pl.when(pl.program_id(0) > 0)
    def _():
        out_ref[...] += total


def weight_gradient(chunks, width, block, per_dst):
    labels = chunks[0][1].shape[1]
    all_labels = labels * per_dst
    devs = chunks[0][0].shape[0]
    rows = sum(grad.shape[0] for _, grad in chunks)
    flat = [a for chunk in chunks for a in chunk]
    specs = []
    for x, grad in chunks:
        specs.append(pl.BlockSpec((block,) + x.shape[1:], lambda i: (i, 0, 0)))
        specs.append(pl.BlockSpec((grad.shape[0] * block // devs, labels), lambda i: (i, 0)))
    return pl.pallas_call(
        functools.partial(weight_kernel, per_dst=per_dst),
        grid=(devs // block,),
        out_shape=jax.ShapeDtypeStruct((all_labels, width), F32),
        in_specs=specs,
        out_specs=whole((all_labels, width)),
        compiler_params=PARAMS,
        cost_estimate=pl.CostEstimate(
            flops=2 * rows * all_labels * width,
            bytes_accessed=2 * rows * (width + all_labels) + 4 * all_labels * width,
            transcendentals=0,
        ),
        name="weight_gradient",
    )(*flat)


def combine_kernel(ret_ref, *refs, order, picks, parts, added, width, steps):
    pick_refs, refs = refs[:picks], refs[picks:]
    add_refs, refs = dict(zip(added, refs[: len(added)])), refs[len(added) :]
    out_refs, ret = refs[: sum(parts)], refs[sum(parts)]
    held, sems = refs[sum(parts) + 1 : -1], refs[-1]
    dsts = ret_ref.shape[0] // steps
    queries = held[0].shape[2]
    rows = dsts * TILE
    over_rows = (((0,), (0,)), ((), ()))
    ats = [pl.ds(step * dsts, dsts) for step in range(steps)]
    pick_copies = [
        pltpu.make_async_copy(ref, place, sems.at[steps + i])
        for i, (ref, place) in enumerate(zip(pick_refs, held))
    ]
    ret_copies = [
        pltpu.make_async_copy(ret_ref.at[at], ret.at[at], sems.at[step]) for step, at in enumerate(ats)
    ]
    for copy in pick_copies + ret_copies:
        copy.start()
    for copy in pick_copies:
        copy.wait()
    totals = [None] * len(order)
    for step, at in enumerate(ats):
        ret_copies[step].wait()
        tiles, last = load_tiles(ret[at])
        for source, (which, index) in enumerate(order):
            pick = held[which][index, pl.ds(step * rows, rows), :]
            x = tiles[source].reshape(rows, width).astype(BF16)
            loss = jnp.dot(last, unit_row(source), preferred_element_type=F32).astype(BF16)
            x = jnp.concatenate([x, loss], axis=1)
            out = lax.dot_general(pick, x, over_rows, preferred_element_type=F32)
            totals[source] = out if step == 0 else totals[source] + out
    first = 0
    for source, count in enumerate(parts):
        out = totals[source]
        if source in add_refs:
            out = out + add_refs[source][...].astype(F32)
        part = queries // count
        for i in range(count):
            out_refs[first + i][...] = out[i * part : (i + 1) * part].astype(BF16)
        first += count


def combine(ret, picks, order, parts, width, arrived=(), params=SMALL):
    queries = picks[0].shape[2]
    shapes = [(queries // count, width + LANES) for count in parts for _ in range(count)]
    added = [a for _, a in arrived]
    steps = 2
    return pl.pallas_call(
        functools.partial(
            combine_kernel,
            order=order,
            picks=len(picks),
            parts=parts,
            added=[i for i, _ in arrived],
            width=width,
            steps=steps,
        ),
        out_shape=[jax.ShapeDtypeStruct(shape, BF16) for shape in shapes],
        in_specs=[IN_HBM] * (1 + len(picks)) + [IN_VMEM] * len(added),
        out_specs=[IN_VMEM] * len(shapes),
        scratch_shapes=[pltpu.VMEM(ret.shape, BF16)]
        + [pltpu.VMEM(pick.shape, BF16) for pick in picks]
        + [pltpu.SemaphoreType.DMA((steps + len(picks),))],
        compiler_params=params,
        name="combine",
    )(ret, *picks, *added)


def add(a, b):
    return (a.astype(F32) + b.astype(F32)).astype(BF16)


def add_half(a, half, second):
    zero = jnp.zeros_like(half)
    return add(a, jnp.concatenate([zero, half] if second else [half, zero], axis=0))


def overflow(encodings, weights, label_count, matched, positive):
    queries, width = encodings.shape
    top = matched.shape[1]
    per_dst = label_count.shape[0]
    groups, dsts = lax.axis_size("grp"), lax.axis_size("dev")
    receivers = groups * dsts
    labels = weights.shape[0] // per_dst
    me = lax.axis_index("grp")
    flat = matched.reshape(-1)
    item = jnp.arange(queries * top, dtype=jnp.int32)
    same = (flat[:, None] == flat[None, :]) & (item[None, :] < item[:, None])
    second = jnp.any(same, axis=1, keepdims=True)
    to = flat[:, None] // per_dst == jnp.arange(receivers)[None, :]
    full = jnp.sum(to, axis=0, keepdims=True) > SLOTS
    late = to & full & second & (flat % per_dst == per_dst - 1)[:, None]
    value = jnp.where(late, positive.reshape(-1, 1) + 1, 0).reshape(queries, top, receivers)
    value = jnp.sum(value, axis=1).astype(BF16)
    pick = (value > 0).astype(BF16)

    def exchange(rows, extra):
        extra = jnp.broadcast_to(extra.astype(BF16), (receivers, LANES))
        v = jnp.concatenate([rows, extra], axis=1)
        v = v.reshape(groups, dsts, width + LANES)
        got = v
        for k in range(1, groups):
            there = lax.dynamic_index_in_dim(v, (me + k) % groups, 0, keepdims=False)
            there = lax.ppermute(there, "grp", [(i, (i + k) % groups) for i in range(groups)])
            got = lax.dynamic_update_index_in_dim(got, there, (me - k) % groups, 0)
        v = lax.all_to_all(got, "dev", split_axis=1, concat_axis=1, tiled=True)
        v = v.reshape(receivers, width + LANES)
        return v[:, 0:width], v[:, width : width + 1]

    turned = (((0,), (0,)), ((), ()))
    rows = lax.dot_general(pick, encodings, turned, preferred_element_type=F32).astype(BF16)
    rows, want = exchange(rows, jnp.sum(value.astype(F32), axis=0)[:, None])
    last = weights[(per_dst - 1) * labels :]
    scores = lax.dot_general(rows, last, (((1,), (1,)), ((), ())), preferred_element_type=F32)
    index = jnp.arange(labels, dtype=jnp.int32)[None, :]
    valid = (index < label_count[per_dst - 1]) & (want > 0)
    target = ((index + 1).astype(F32) == want.astype(F32)).astype(F32)
    soft = jnp.maximum(scores, 0.0) + jnp.log(1.0 + jnp.exp(-jnp.abs(scores)))
    loss = jnp.sum(jnp.where(valid, soft - target * scores, 0.0), axis=1, keepdims=True)
    grad = jnp.where(valid, jax.nn.sigmoid(scores) - target, 0.0).astype(BF16)
    part = jnp.dot(grad, last, preferred_element_type=F32).astype(BF16)
    weight_part = lax.dot_general(grad, rows, turned, preferred_element_type=F32)
    part, loss = exchange(part, loss)
    enc_part = jnp.dot(pick, part, preferred_element_type=F32)
    loss_part = jnp.dot(pick, loss, preferred_element_type=F32)[:, 0]
    return enc_part, loss_part, weight_part


def finish_kernel(mine_ref, lower_ref, upper_ref, grad_ref, loss_ref, *, scale):
    width = grad_ref.shape[1]
    total = mine_ref[...].astype(F32) + lower_ref[...].astype(F32) + upper_ref[...].astype(F32)
    grad_ref[...] = total[:, 0:width].astype(BF16)
    loss_ref[...] = total[:, width:].T[0:1] * scale


def finish(mine, to_lower, to_upper, scale):
    queries, wide = mine.shape
    width = wide - LANES
    return pl.pallas_call(
        functools.partial(finish_kernel, scale=scale),
        out_shape=(
            jax.ShapeDtypeStruct((queries, width), BF16),
            jax.ShapeDtypeStruct((1, queries), F32),
        ),
        in_specs=[IN_VMEM] * 3,
        out_specs=[IN_VMEM] * 2,
        compiler_params=SMALL,
        name="finish",
    )(mine, to_lower, to_upper)


def per_device(encodings, label_weights, label_count, matched, positive):
    queries, width = encodings.shape
    top = matched.shape[1]
    per_dst = label_count.shape[0]
    dsts = lax.axis_size("dev")
    groups = lax.axis_size("grp")
    labels = label_weights.shape[0] // per_dst
    half = queries // 2
    reach = groups // 2
    up_pairs = [(i, (i + 1) % groups) for i in range(groups)]
    down_pairs = [(i, (i - 1) % groups) for i in range(groups)]

    def up(v):
        return lax.ppermute(v, "grp", up_pairs)

    def down(v):
        return lax.ppermute(v, "grp", down_pairs)

    def exchange(v):
        return lax.all_to_all(v, "dev", split_axis=0, concat_axis=0, tiled=True)

    me = lax.axis_index("grp").astype(jnp.int32).reshape(1)
    own = prepare(encodings, matched, positive, per_dst * dsts, per_dst, groups * dsts)
    lower, upper = [own], [own]
    for _ in range(1, reach):
        lower.append(up(lower[-1]))
        upper.append(down(upper[-1]))
    across = (up(lower[-1][:half]), down(upper[-1][half:]))
    chunks = [
        [(own,)],
        [(v[k],) for k in range(1, reach - 1) for v in (lower, upper)],
        [(lower[-1],), (upper[-1],), across],
    ]
    picks, got = [], []
    seen = jnp.zeros((TILE, LANES), F32)
    for sources in chunks:
        send, pick, seen = dispatch(sources, me, seen, dsts, per_dst, top)
        if got:
            send, got[-1] = lax.optimization_barrier((send, got[-1]))
        got.append(exchange(send))
        picks.append(pick)

    block = min(16, dsts)
    mid = list(range(len(chunks[1])))
    part_own, grad_own, _ = score(got[0], label_weights, label_count, block, [[0]])
    part_near, part_mid, grad_mid, _ = score(
        got[1], label_weights, label_count, block, [mid[:2], mid[2:]], part_own
    )
    part_mid, part_near = lax.optimization_barrier((part_mid, part_near))
    part_far, grad_far, over = score(got[2], label_weights, label_count, block, [[0, 1, 2]], part_mid)
    back_far = exchange(part_far)
    weight_grad = weight_gradient(list(zip(got, [grad_own, grad_mid, grad_far])), width, block, per_dst)
    part_near, back_far, weight_grad = lax.optimization_barrier((part_near, back_far, weight_grad))
    back_near = exchange(part_near)

    order = [(0, i) for i in mid[2:]] + [(1, 0), (1, 1), (1, 2)]
    parts = [1] * (len(order) - 1) + [2]
    sums = list(combine(back_far, picks[1:], order, parts, width, (), PARAMS))
    to_lower, to_upper = down(sums[-2]), up(sums[-1])
    sums = sums[:-2]
    sums[-2:] = [add_half(sums[-2], to_lower, False), add_half(sums[-1], to_upper, True)]
    to_lower, to_upper = down(sums[-2]), up(sums[-1])
    sums = sums[:-2]
    while sums:
        to_lower, to_upper = down(add(sums[-2], to_lower)), up(add(sums[-1], to_upper))
        sums = sums[:-2]
    order = [(0, 0), (1, 0), (1, 1)]
    arrived = ((1, to_lower), (2, to_upper))
    mine, a, b = combine(back_near, picks[:2], order, [1, 1, 1], width, arrived)
    to_lower, to_upper = down(a), up(b)
    scale = 1.0 / (top * labels)

    def plain(mine, to_lower, to_upper, weight_grad):
        enc_grad, query_loss = finish(mine, to_lower, to_upper, scale)
        return enc_grad, query_loss.reshape(queries), weight_grad

    def with_overflow(mine, to_lower, to_upper, weight_grad):
        enc_part, loss_part, weight_part = overflow(
            encodings, label_weights, label_count, matched, positive
        )
        total = mine.astype(F32) + to_lower.astype(F32) + to_upper.astype(F32)
        enc_grad = (total[:, 0:width] + enc_part).astype(BF16)
        query_loss = (total[:, width] + loss_part) * scale
        return enc_grad, query_loss, weight_grad.at[(per_dst - 1) * labels :].add(weight_part)

    enc_grad, query_loss, weight_grad = lax.cond(
        over[0, LANES - 1] > 0.0, with_overflow, plain, mine, to_lower, to_upper, weight_grad
    )
    return enc_grad, query_loss, weight_grad


def solution(mesh):
    in_specs = (
        P(("grp", "dev"), None),
        P(("grp", "dev"), None),
        P(("grp", "dev")),
        P(("grp", "dev"), None),
        P(("grp", "dev"), None),
    )
    out_specs = (P(("grp", "dev"), None), P(("grp", "dev")), P(("grp", "dev"), None))
    return jax.shard_map(
        per_device, mesh=mesh, in_specs=in_specs, out_specs=out_specs, check_vma=False
    )
```

```python
import functools

import jax
import jax.numpy as jnp
from jax import lax
from jax.experimental import pallas as pl
from jax.experimental.pallas import tpu as pltpu
from jax.sharding import PartitionSpec as P

F32 = jnp.float32
BF16 = jnp.bfloat16
LANES = 128
TILE = 8
META = 16
PARAMS = pltpu.CompilerParams(vmem_limit_bytes=63 * 1024 * 1024)
SMALL = pltpu.CompilerParams(vmem_limit_bytes=28 * 1024 * 1024)
IN_HBM = pl.BlockSpec(memory_space=pltpu.HBM)
IN_VMEM = pl.BlockSpec(memory_space=pltpu.VMEM)


def iota(shape, dim):
    return lax.broadcasted_iota(jnp.int32, shape, dim)


def whole(shape):
    return pl.BlockSpec(shape, lambda i: (0,) * len(shape))


def unit_row(row):
    return (iota((LANES, LANES), 0) == row).astype(BF16)


def unit_column(shape, column):
    return (iota(shape, 1) == column).astype(BF16)


def store_tiles(ref, first, rows, at=slice(None)):
    for k in range(0, rows.shape[2] // LANES, 2):
        left = rows[:, :, k * LANES : (k + 1) * LANES]
        right = rows[:, :, (k + 1) * LANES : (k + 2) * LANES]
        ref[at, pl.ds(first + k * TILE, 2 * TILE), :] = jnp.concatenate([left, right], axis=1).astype(BF16)


def load_tiles(held, width):
    devs, tile_rows, _ = held.shape
    per_source = width // LANES
    sources = (tile_rows // TILE - 1) // per_source
    tiles = held.astype(F32).reshape(devs, tile_rows // TILE, TILE, LANES)
    rows = [
        jnp.concatenate([tiles[:, s * per_source + k] for k in range(per_source)], axis=2)
        for s in range(sources)
    ]
    return rows, tiles[:, sources * per_source].reshape(devs * TILE, LANES).astype(BF16)


def prepare_kernel(enc_ref, matched_ref, positive_ref, out_ref, held, sems, *, in_group):
    queries = enc_ref.shape[0]
    top = matched_ref.shape[0]
    copies = [
        pltpu.make_async_copy(matched_ref, held.at[0], sems.at[0]),
        pltpu.make_async_copy(positive_ref, held.at[1], sems.at[1]),
        pltpu.make_async_copy(enc_ref, out_ref.at[pl.ds(0, queries)], sems.at[2]),
    ]
    for copy in copies:
        copy.start()
    copies[0].wait()
    copies[1].wait()
    matched = held[0]
    group = matched // in_group
    parts = (group, matched - group * in_group, held[1])
    meta = jnp.concatenate([part.astype(F32) for part in parts], axis=1)
    meta = jnp.concatenate([meta, jnp.zeros((top, out_ref.shape[1] - meta.shape[1]), F32)], axis=1)
    if META > top:
        meta = jnp.concatenate([meta, jnp.zeros((META - top, meta.shape[1]), F32)], axis=0)
    out_ref[queries:] = meta.astype(BF16)
    copies[2].wait()


def prepare(encodings, matched, positive, in_group):
    queries, width = encodings.shape
    top = matched.shape[1]
    return pl.pallas_call(
        functools.partial(prepare_kernel, in_group=in_group),
        out_shape=jax.ShapeDtypeStruct((queries + META, width), BF16),
        in_specs=[IN_HBM] * 3,
        out_specs=IN_VMEM,
        scratch_shapes=[pltpu.VMEM((2, top, queries), jnp.int32), pltpu.SemaphoreType.DMA((3,))],
        compiler_params=PARAMS,
        name="prepare",
    )(encodings, matched.T, positive.T)


def dispatch_kernel(grp_ref, *refs, parts, top, per_dst, steps):
    x_refs, (send_ref, pick_ref, send, picks, sems) = refs[:-5], refs[-5:]
    width = x_refs[0].shape[1]
    queries = pick_ref.shape[2]
    sources = len(parts)
    dsts = send_ref.shape[0] // steps
    rows = dsts * TILE
    me = grp_ref[0].astype(F32)
    row = iota((rows, queries), 0)
    rank = ((row // per_dst) % 2).astype(F32)
    before = (iota((queries, queries), 0) < iota((queries, queries), 1)).astype(BF16)
    blocks, keys, wants, first = [], [], [], 0
    for count in parts:
        x = jnp.concatenate([r[...] for r in x_refs[first : first + count]], axis=0)
        first += count
        meta = x[queries:].astype(F32)[0:top]
        group, local, slot = [meta[:, i * queries : (i + 1) * queries] for i in range(3)]
        blocks.append(x[0:queries])
        keys.append(jnp.where(group == me, local, -1.0).astype(BF16))
        wants.append((slot + 1.0).astype(BF16))
    copies = []
    for step in range(steps):
        cluster = ((row // TILE + step * dsts) * per_dst + row % per_dst).astype(F32).astype(BF16)
        at, at_rows = pl.ds(step * dsts, dsts), pl.ds(step * rows, rows)
        last = jnp.zeros((rows, LANES), F32)
        for source in range(sources):
            value = jnp.zeros((rows, queries), BF16)
            for t in range(top):
                same = cluster == keys[source][t : t + 1]
                value = value + jnp.where(same, wants[source][t : t + 1], jnp.zeros((), BF16))
            hit = (value > 0.0).astype(BF16)
            earlier = jnp.dot(hit, before, preferred_element_type=F32)
            value = jnp.where(earlier == rank, value.astype(F32), 0.0)
            pick = (value > 0.0).astype(BF16)
            picks[source, at_rows, :] = pick
            out = jnp.dot(pick, blocks[source], preferred_element_type=F32)
            store_tiles(send, source * width // LANES * TILE, out.reshape(dsts, TILE, width), at)
            place = unit_column((queries, LANES), source)
            last = last + jnp.dot(value.astype(BF16), place, preferred_element_type=F32)
        end = sources * width // LANES * TILE
        send[at, end:, :] = last.reshape(dsts, TILE, LANES).astype(BF16)
        copies.append(pltpu.make_async_copy(send.at[at], send_ref.at[at], sems.at[0, step]))
        copies.append(
            pltpu.make_async_copy(picks.at[:, at_rows], pick_ref.at[:, at_rows], sems.at[1, step])
        )
        copies[-2].start()
        copies[-1].start()
    for copy in copies:
        copy.wait()


def dispatch(sources, grp, dsts, per_dst, top):
    flat = [block for blocks in sources for block in blocks]
    queries = sum(block.shape[0] for block in sources[0]) - META
    width = flat[0].shape[1]
    send = (dsts, (len(sources) * width // LANES + 1) * TILE, LANES)
    pick = (len(sources), dsts * TILE, queries)
    steps = 2
    return pl.pallas_call(
        functools.partial(
            dispatch_kernel,
            parts=[len(blocks) for blocks in sources],
            top=top,
            per_dst=per_dst,
            steps=steps,
        ),
        out_shape=(jax.ShapeDtypeStruct(send, BF16), jax.ShapeDtypeStruct(pick, BF16)),
        in_specs=[pl.BlockSpec(memory_space=pltpu.SMEM)] + [IN_VMEM] * len(flat),
        out_specs=[IN_HBM, IN_HBM],
        scratch_shapes=[
            pltpu.VMEM(send, BF16),
            pltpu.VMEM(pick, BF16),
            pltpu.SemaphoreType.DMA((2, steps)),
        ],
        compiler_params=SMALL,
        name="dispatch",
    )(grp, *flat)


def own_columns(grad, per_dst):
    own = iota(grad.shape, 0) % per_dst
    return jnp.concatenate([jnp.where(own == cl, grad, 0.0) for cl in range(per_dst)], axis=1).astype(BF16)


def score_kernel(count_ref, x_ref, w_ref, *refs, per_dst, carried, outs):
    carry_ref, ret_refs, grad_ref = refs[0], refs[1 if carried else 0 : -1], refs[-1]
    devs = x_ref.shape[0]
    all_labels, width = w_ref.shape
    labels = all_labels // per_dst
    per_source = width // LANES * TILE
    tiles, last = load_tiles(x_ref[...], width)
    sources = len(tiles)
    rows = devs * sources * TILE
    x = jnp.concatenate([t.reshape(devs, 1, TILE, width) for t in tiles], axis=1)
    x = x.reshape(rows, width).astype(BF16)
    want = jnp.concatenate(
        [
            jnp.dot(last, unit_row(s), preferred_element_type=F32).reshape(devs, 1, TILE, LANES)
            for s in range(sources)
        ],
        axis=1,
    ).reshape(rows, LANES)
    scores = lax.dot_general(
        x, w_ref[...], (((1,), (1,)), ((), ())), preferred_element_type=F32
    )
    own = iota((rows, labels), 0) % per_dst
    label = iota((rows, labels), 1)
    s = scores[:, 0:labels]
    count = jnp.full((rows, labels), count_ref[0], jnp.int32)
    for cl in range(1, per_dst):
        s = jnp.where(own == cl, scores[:, cl * labels : (cl + 1) * labels], s)
        count = jnp.where(own == cl, count_ref[cl], count)
    valid = label < count
    target = (label.astype(F32) + 1.0) == want
    small = jnp.exp(-jnp.abs(s))
    soft = jnp.maximum(s, 0.0) + jnp.log(1.0 + small)
    term = jnp.where(valid, soft - jnp.where(target, s, 0.0), 0.0)
    loss = jnp.sum(term, axis=1, keepdims=True).reshape(devs, sources, TILE, 1)
    sig = jnp.where(s >= 0.0, 1.0, small) / (1.0 + small)
    grad = jnp.where(valid, sig - jnp.where(target, 1.0, 0.0), 0.0)
    grad_ref[...] = grad.astype(BF16)
    part = jnp.dot(own_columns(grad, per_dst), w_ref[...], preferred_element_type=F32)
    part = part.reshape(devs, sources, TILE, width)
    lane = iota((devs, TILE, LANES), 2)
    for i, (ret_ref, members) in enumerate(zip(ret_refs, outs)):
        before = carried if i == 0 else 0
        last = jnp.zeros((devs, TILE, LANES), F32)
        if before:
            end = before * per_source
            ret_ref[:, 0:end, :] = carry_ref[:, 0:end, :]
            last = carry_ref[:, end:, :].astype(F32)
        for j, source in enumerate(members):
            store_tiles(ret_ref, (before + j) * per_source, part[:, source])
            last = jnp.where(lane == before + j, loss[:, source], last)
        ret_ref[:, (before + len(members)) * per_source :, :] = last.astype(BF16)


def sources_of(x, width):
    return (x.shape[1] // TILE - 1) * LANES // width


def score(x, weights, count, block, outs, carry=None, params=PARAMS):
    devs, tile_rows, _ = x.shape
    per_dst = count.shape[0]
    all_labels, width = weights.shape
    labels = all_labels // per_dst
    slots = sources_of(x, width) * TILE
    carried = sources_of(carry, width) if carry is not None else 0
    sizes = [len(members) + (carried if i == 0 else 0) for i, members in enumerate(outs)]
    ret_rows = [(size * width // LANES + 1) * TILE for size in sizes]

    def by_dev(rows):
        return pl.BlockSpec((block, rows, LANES), lambda i: (i, 0, 0))

    return pl.pallas_call(
        functools.partial(score_kernel, per_dst=per_dst, carried=carried, outs=outs),
        grid=(devs // block,),
        out_shape=[jax.ShapeDtypeStruct((devs, r, LANES), BF16) for r in ret_rows]
        + [jax.ShapeDtypeStruct((devs * slots, labels), BF16)],
        in_specs=[
            pl.BlockSpec(memory_space=pltpu.SMEM),
            by_dev(tile_rows),
            whole((all_labels, width)),
        ]
        + ([by_dev(carry.shape[1])] if carried else []),
        out_specs=[by_dev(r) for r in ret_rows]
        + [pl.BlockSpec((block * slots, labels), lambda i: (i, 0))],
        compiler_params=params,
        cost_estimate=pl.CostEstimate(
            flops=4 * devs * slots * all_labels * width,
            bytes_accessed=4 * devs * slots * (width + labels) + 2 * all_labels * width,
            transcendentals=0,
        ),
        name="score",
    )(count, x, weights, *([carry] if carried else []))


def weight_kernel(*refs, per_dst):
    out_ref = refs[-1]
    width = out_ref.shape[1]
    total = None
    for x_ref, grad_ref in zip(refs[0:-1:2], refs[1:-1:2]):
        tiles, _ = load_tiles(x_ref[...], width)
        devs = x_ref.shape[0]
        x = jnp.concatenate([t.reshape(devs, 1, TILE, width) for t in tiles], axis=1)
        x = x.reshape(devs * len(tiles) * TILE, width).astype(BF16)
        grad = own_columns(grad_ref[...].astype(F32), per_dst)
        part = lax.dot_general(
            grad, x, (((0,), (0,)), ((), ())), preferred_element_type=F32
        )
        total = part if total is None else total + part

    @pl.when(pl.program_id(0) == 0)
    def _():
        out_ref[...] = total

    @pl.when(pl.program_id(0) > 0)
    def _():
        out_ref[...] += total


def weight_gradient(chunks, width, block, per_dst):
    labels = chunks[0][1].shape[1]
    all_labels = labels * per_dst
    devs = chunks[0][0].shape[0]
    rows = sum(grad.shape[0] for _, grad in chunks)
    flat = [a for chunk in chunks for a in chunk]
    specs = []
    for x, grad in chunks:
        specs.append(pl.BlockSpec((block,) + x.shape[1:], lambda i: (i, 0, 0)))
        specs.append(pl.BlockSpec((grad.shape[0] * block // devs, labels), lambda i: (i, 0)))
    return pl.pallas_call(
        functools.partial(weight_kernel, per_dst=per_dst),
        grid=(devs // block,),
        out_shape=jax.ShapeDtypeStruct((all_labels, width), F32),
        in_specs=specs,
        out_specs=whole((all_labels, width)),
        compiler_params=PARAMS,
        cost_estimate=pl.CostEstimate(
            flops=2 * rows * all_labels * width,
            bytes_accessed=2 * rows * (width + all_labels) + 4 * all_labels * width,
            transcendentals=0,
        ),
        name="weight_gradient",
    )(*flat)


def combine_kernel(ret_ref, *refs, order, picks, parts, added, width, steps):
    pick_refs, refs = refs[:picks], refs[picks:]
    add_refs, refs = dict(zip(added, refs[: len(added)])), refs[len(added) :]
    out_refs, ret = refs[: sum(parts)], refs[sum(parts)]
    held, sems = refs[sum(parts) + 1 : -1], refs[-1]
    dsts = ret_ref.shape[0] // steps
    queries = held[0].shape[2]
    rows = dsts * TILE
    over_rows = (((0,), (0,)), ((), ()))
    ats = [pl.ds(step * dsts, dsts) for step in range(steps)]
    pick_copies = [
        pltpu.make_async_copy(ref, place, sems.at[steps + i])
        for i, (ref, place) in enumerate(zip(pick_refs, held))
    ]
    ret_copies = [
        pltpu.make_async_copy(ret_ref.at[at], ret.at[at], sems.at[step]) for step, at in enumerate(ats)
    ]
    for copy in pick_copies + ret_copies:
        copy.start()
    for copy in pick_copies:
        copy.wait()
    totals = [None] * len(order)
    for step, at in enumerate(ats):
        ret_copies[step].wait()
        tiles, last = load_tiles(ret[at], width)
        for source, (which, index) in enumerate(order):
            pick = held[which][index, pl.ds(step * rows, rows), :]
            x = tiles[source].reshape(rows, width).astype(BF16)
            loss = jnp.dot(last, unit_row(source), preferred_element_type=F32).astype(BF16)
            x = jnp.concatenate([x, loss], axis=1)
            out = lax.dot_general(pick, x, over_rows, preferred_element_type=F32)
            totals[source] = out if step == 0 else totals[source] + out
    first = 0
    for source, count in enumerate(parts):
        out = totals[source]
        if source in add_refs:
            out = out + add_refs[source][...].astype(F32)
        part = queries // count
        for i in range(count):
            out_refs[first + i][...] = out[i * part : (i + 1) * part].astype(BF16)
        first += count


def combine(ret, picks, order, parts, width, arrived=(), params=SMALL):
    queries = picks[0].shape[2]
    shapes = [(queries // count, width + LANES) for count in parts for _ in range(count)]
    added = [a for _, a in arrived]
    steps = 1
    return pl.pallas_call(
        functools.partial(
            combine_kernel,
            order=order,
            picks=len(picks),
            parts=parts,
            added=[i for i, _ in arrived],
            width=width,
            steps=steps,
        ),
        out_shape=[jax.ShapeDtypeStruct(shape, BF16) for shape in shapes],
        in_specs=[IN_HBM] * (1 + len(picks)) + [IN_VMEM] * len(added),
        out_specs=[IN_VMEM] * len(shapes),
        scratch_shapes=[pltpu.VMEM(ret.shape, BF16)]
        + [pltpu.VMEM(pick.shape, BF16) for pick in picks]
        + [pltpu.SemaphoreType.DMA((steps + len(picks),))],
        compiler_params=params,
        name="combine",
    )(ret, *picks, *added)


def add(a, b):
    return (a.astype(F32) + b.astype(F32)).astype(BF16)


def add_half(a, half, second):
    zero = jnp.zeros_like(half)
    return add(a, jnp.concatenate([zero, half] if second else [half, zero], axis=0))


def finish_kernel(mine_ref, lower_ref, upper_ref, grad_ref, loss_ref, grad, loss, sems, *, scale):
    width = grad_ref.shape[1]
    total = mine_ref[...].astype(F32) + lower_ref[...].astype(F32) + upper_ref[...].astype(F32)
    grad[...] = total[:, 0:width].astype(BF16)
    grad_copy = pltpu.make_async_copy(grad, grad_ref, sems.at[0])
    grad_copy.start()
    loss[...] = total[:, width:].T[0:1] * scale
    loss_copy = pltpu.make_async_copy(loss, loss_ref, sems.at[1])
    loss_copy.start()
    grad_copy.wait()
    loss_copy.wait()


def finish(mine, to_lower, to_upper, scale):
    queries, wide = mine.shape
    width = wide - LANES
    return pl.pallas_call(
        functools.partial(finish_kernel, scale=scale),
        out_shape=(
            jax.ShapeDtypeStruct((queries, width), BF16),
            jax.ShapeDtypeStruct((1, queries), F32),
        ),
        in_specs=[IN_VMEM] * 3,
        out_specs=[IN_HBM] * 2,
        scratch_shapes=[
            pltpu.VMEM((queries, width), BF16),
            pltpu.VMEM((1, queries), F32),
            pltpu.SemaphoreType.DMA((2,)),
        ],
        compiler_params=SMALL,
        name="finish",
    )(mine, to_lower, to_upper)


def per_device(encodings, label_weights, label_count, matched, positive):
    queries, width = encodings.shape
    top = matched.shape[1]
    per_dst = label_count.shape[0]
    dsts = lax.axis_size("dev")
    groups = lax.axis_size("grp")
    labels = label_weights.shape[0] // per_dst
    half = queries // 2
    reach = groups // 2
    up_pairs = [(i, (i + 1) % groups) for i in range(groups)]
    down_pairs = [(i, (i - 1) % groups) for i in range(groups)]

    def up(v):
        return lax.ppermute(v, "grp", up_pairs)

    def down(v):
        return lax.ppermute(v, "grp", down_pairs)

    def exchange(v):
        return lax.all_to_all(v, "dev", split_axis=0, concat_axis=0, tiled=True)

    me = lax.axis_index("grp").astype(jnp.int32).reshape(1)
    own = prepare(encodings, matched, positive, per_dst * dsts)
    lower, upper = [own], [own]
    for _ in range(1, reach):
        lower.append(up(lower[-1]))
        upper.append(down(upper[-1]))
    across = (up(lower[-1][:half]), down(upper[-1][half:]))
    chunks = [
        [(own,)],
        [(v[k],) for k in range(1, reach - 1) for v in (lower, upper)],
        [(lower[-1],), (upper[-1],), across],
    ]
    picks, got = [], []
    for sources in chunks:
        send, pick = dispatch(sources, me, dsts, per_dst, top)
        if got:
            send, got[-1] = lax.optimization_barrier((send, got[-1]))
        got.append(exchange(send))
        picks.append(pick)

    block = min(16, dsts)
    mid = list(range(len(chunks[1])))
    part_own, grad_own = score(got[0], label_weights, label_count, block, [[0]], None, SMALL)
    part_near, part_mid, grad_mid = score(
        got[1], label_weights, label_count, block, [mid[:2], mid[2:]], part_own
    )
    part_mid, part_near = lax.optimization_barrier((part_mid, part_near))
    part_far, grad_far = score(got[2], label_weights, label_count, block, [[0, 1, 2]], part_mid)
    back_far = exchange(part_far)
    weight_grad = weight_gradient(list(zip(got, [grad_own, grad_mid, grad_far])), width, block, per_dst)
    part_near, back_far, weight_grad = lax.optimization_barrier((part_near, back_far, weight_grad))
    back_near = exchange(part_near)

    order = [(0, i) for i in mid[2:]] + [(1, 0), (1, 1), (1, 2)]
    parts = [1] * (len(order) - 1) + [2]
    sums = list(combine(back_far, picks[1:], order, parts, width, (), PARAMS))
    to_lower, to_upper = down(sums[-2]), up(sums[-1])
    sums = sums[:-2]
    sums[-2:] = [add_half(sums[-2], to_lower, False), add_half(sums[-1], to_upper, True)]
    to_lower, to_upper = down(sums[-2]), up(sums[-1])
    sums = sums[:-2]
    while sums:
        to_lower, to_upper = down(add(sums[-2], to_lower)), up(add(sums[-1], to_upper))
        sums = sums[:-2]
    order = [(0, 0), (1, 0), (1, 1)]
    arrived = ((1, to_lower), (2, to_upper))
    mine, a, b = combine(back_near, picks[:2], order, [1, 1, 1], width, arrived)
    to_lower, to_upper = down(a), up(b)
    enc_grad, query_loss = finish(mine, to_lower, to_upper, 1.0 / (top * labels))
    query_loss = query_loss.reshape(queries)
    return enc_grad, query_loss, weight_grad


def solution(mesh):
    in_specs = (
        P(("grp", "dev"), None),
        P(("grp", "dev"), None),
        P(("grp", "dev")),
        P(("grp", "dev"), None),
        P(("grp", "dev"), None),
    )
    out_specs = (P(("grp", "dev"), None), P(("grp", "dev")), P(("grp", "dev"), None))
    return jax.shard_map(
        per_device, mesh=mesh, in_specs=in_specs, out_specs=out_specs, check_vma=False
    )
```

```python
import functools

import jax
import jax.numpy as jnp
from jax import lax
from jax.experimental import pallas as pl
from jax.experimental.pallas import tpu as pltpu
from jax.sharding import PartitionSpec as P

F32 = jnp.float32
BF16 = jnp.bfloat16
LANES = 128
TILE = 8
META = 16
PARAMS = pltpu.CompilerParams(vmem_limit_bytes=63 * 1024 * 1024)
SMALL = pltpu.CompilerParams(vmem_limit_bytes=28 * 1024 * 1024)
IN_HBM = pl.BlockSpec(memory_space=pltpu.HBM)
IN_VMEM = pl.BlockSpec(memory_space=pltpu.VMEM)


def iota(shape, dim):
    return lax.broadcasted_iota(jnp.int32, shape, dim)


def whole(shape):
    return pl.BlockSpec(shape, lambda i: (0,) * len(shape))


def unit_row(row):
    return (iota((LANES, LANES), 0) == row).astype(BF16)


def unit_column(shape, column):
    return (iota(shape, 1) == column).astype(BF16)


def store_tiles(ref, first, rows, at=slice(None)):
    for k in range(0, rows.shape[2] // LANES, 2):
        left = rows[:, :, k * LANES : (k + 1) * LANES]
        right = rows[:, :, (k + 1) * LANES : (k + 2) * LANES]
        ref[at, pl.ds(first + k * TILE, 2 * TILE), :] = jnp.concatenate([left, right], axis=1).astype(BF16)


def load_tiles(held, width):
    devs, tile_rows, _ = held.shape
    per_source = width // LANES
    sources = (tile_rows // TILE - 1) // per_source
    tiles = held.astype(F32).reshape(devs, tile_rows // TILE, TILE, LANES)
    rows = [
        jnp.concatenate([tiles[:, s * per_source + k] for k in range(per_source)], axis=2)
        for s in range(sources)
    ]
    return rows, tiles[:, sources * per_source].reshape(devs * TILE, LANES).astype(BF16)


def prepare_kernel(enc_ref, matched_ref, positive_ref, out_ref, held, sems, *, in_group):
    queries = enc_ref.shape[0]
    top = matched_ref.shape[0]
    copies = [
        pltpu.make_async_copy(matched_ref, held.at[0], sems.at[0]),
        pltpu.make_async_copy(positive_ref, held.at[1], sems.at[1]),
        pltpu.make_async_copy(enc_ref, out_ref.at[pl.ds(0, queries)], sems.at[2]),
    ]
    for copy in copies:
        copy.start()
    copies[0].wait()
    copies[1].wait()
    matched = held[0]
    group = matched // in_group
    parts = (group, matched - group * in_group, held[1])
    meta = jnp.concatenate([part.astype(F32) for part in parts], axis=1)
    meta = jnp.concatenate([meta, jnp.zeros((top, out_ref.shape[1] - meta.shape[1]), F32)], axis=1)
    if META > top:
        meta = jnp.concatenate([meta, jnp.zeros((META - top, meta.shape[1]), F32)], axis=0)
    out_ref[queries:] = meta.astype(BF16)
    copies[2].wait()


def prepare(encodings, matched, positive, in_group):
    queries, width = encodings.shape
    top = matched.shape[1]
    return pl.pallas_call(
        functools.partial(prepare_kernel, in_group=in_group),
        out_shape=jax.ShapeDtypeStruct((queries + META, width), BF16),
        in_specs=[IN_HBM] * 3,
        out_specs=IN_VMEM,
        scratch_shapes=[pltpu.VMEM((2, top, queries), jnp.int32), pltpu.SemaphoreType.DMA((3,))],
        compiler_params=PARAMS,
        name="prepare",
    )(encodings, matched.T, positive.T)


def dispatch_kernel(grp_ref, *refs, parts, top, per_dst, steps):
    x_refs, (send_ref, pick_ref, send, picks, sems) = refs[:-5], refs[-5:]
    width = x_refs[0].shape[1]
    queries = pick_ref.shape[2]
    sources = len(parts)
    dsts = send_ref.shape[0] // steps
    rows = dsts * TILE
    me = grp_ref[0].astype(F32)
    row = iota((rows, queries), 0)
    rank = ((row // per_dst) % 2).astype(F32)
    before = (iota((queries, queries), 0) < iota((queries, queries), 1)).astype(BF16)
    blocks, keys, wants, first = [], [], [], 0
    for count in parts:
        x = jnp.concatenate([r[...] for r in x_refs[first : first + count]], axis=0)
        first += count
        meta = x[queries:].astype(F32)[0:top]
        group, local, slot = [meta[:, i * queries : (i + 1) * queries] for i in range(3)]
        blocks.append(x[0:queries])
        keys.append(jnp.where(group == me, local, -1.0).astype(BF16))
        wants.append((slot + 1.0).astype(BF16))
    copies = []
    for step in range(steps):
        cluster = ((row // TILE + step * dsts) * per_dst + row % per_dst).astype(F32).astype(BF16)
        at, at_rows = pl.ds(step * dsts, dsts), pl.ds(step * rows, rows)
        last = jnp.zeros((rows, LANES), F32)
        for source in range(sources):
            value = jnp.zeros((rows, queries), BF16)
            for t in range(top):
                same = cluster == keys[source][t : t + 1]
                value = value + jnp.where(same, wants[source][t : t + 1], jnp.zeros((), BF16))
            hit = (value > 0.0).astype(BF16)
            earlier = jnp.dot(hit, before, preferred_element_type=F32)
            value = jnp.where(earlier == rank, value.astype(F32), 0.0)
            pick = (value > 0.0).astype(BF16)
            picks[source, at_rows, :] = pick
            out = jnp.dot(pick, blocks[source], preferred_element_type=F32)
            store_tiles(send, source * width // LANES * TILE, out.reshape(dsts, TILE, width), at)
            place = unit_column((queries, LANES), source)
            last = last + jnp.dot(value.astype(BF16), place, preferred_element_type=F32)
        end = sources * width // LANES * TILE
        send[at, end:, :] = last.reshape(dsts, TILE, LANES).astype(BF16)
        copies.append(pltpu.make_async_copy(send.at[at], send_ref.at[at], sems.at[0, step]))
        copies.append(
            pltpu.make_async_copy(picks.at[:, at_rows], pick_ref.at[:, at_rows], sems.at[1, step])
        )
        copies[-2].start()
        copies[-1].start()
    for copy in copies:
        copy.wait()


def dispatch(sources, grp, dsts, per_dst, top):
    flat = [block for blocks in sources for block in blocks]
    queries = sum(block.shape[0] for block in sources[0]) - META
    width = flat[0].shape[1]
    send = (dsts, (len(sources) * width // LANES + 1) * TILE, LANES)
    pick = (len(sources), dsts * TILE, queries)
    steps = 1
    return pl.pallas_call(
        functools.partial(
            dispatch_kernel,
            parts=[len(blocks) for blocks in sources],
            top=top,
            per_dst=per_dst,
            steps=steps,
        ),
        out_shape=(jax.ShapeDtypeStruct(send, BF16), jax.ShapeDtypeStruct(pick, BF16)),
        in_specs=[pl.BlockSpec(memory_space=pltpu.SMEM)] + [IN_VMEM] * len(flat),
        out_specs=[IN_HBM, IN_HBM],
        scratch_shapes=[
            pltpu.VMEM(send, BF16),
            pltpu.VMEM(pick, BF16),
            pltpu.SemaphoreType.DMA((2, steps)),
        ],
        compiler_params=SMALL,
        name="dispatch",
    )(grp, *flat)


def own_columns(grad, per_dst):
    own = iota(grad.shape, 0) % per_dst
    return jnp.concatenate([jnp.where(own == cl, grad, 0.0) for cl in range(per_dst)], axis=1).astype(BF16)


def score_kernel(count_ref, x_ref, w_ref, *refs, per_dst, carried, outs):
    carry_ref, ret_refs, grad_ref = refs[0], refs[1 if carried else 0 : -1], refs[-1]
    devs = x_ref.shape[0]
    all_labels, width = w_ref.shape
    labels = all_labels // per_dst
    per_source = width // LANES * TILE
    tiles, last = load_tiles(x_ref[...], width)
    sources = len(tiles)
    rows = devs * sources * TILE
    x = jnp.concatenate([t.reshape(devs, 1, TILE, width) for t in tiles], axis=1)
    x = x.reshape(rows, width).astype(BF16)
    want = jnp.concatenate(
        [
            jnp.dot(last, unit_row(s), preferred_element_type=F32).reshape(devs, 1, TILE, LANES)
            for s in range(sources)
        ],
        axis=1,
    ).reshape(rows, LANES)
    scores = lax.dot_general(
        x, w_ref[...], (((1,), (1,)), ((), ())), preferred_element_type=F32
    )
    own = iota((rows, labels), 0) % per_dst
    label = iota((rows, labels), 1)
    s = scores[:, 0:labels]
    count = jnp.full((rows, labels), count_ref[0], jnp.int32)
    for cl in range(1, per_dst):
        s = jnp.where(own == cl, scores[:, cl * labels : (cl + 1) * labels], s)
        count = jnp.where(own == cl, count_ref[cl], count)
    valid = label < count
    target = (label.astype(F32) + 1.0) == want
    small = jnp.exp(-jnp.abs(s))
    soft = jnp.maximum(s, 0.0) + jnp.log(1.0 + small)
    term = jnp.where(valid, soft - jnp.where(target, s, 0.0), 0.0)
    loss = jnp.sum(term, axis=1, keepdims=True).reshape(devs, sources, TILE, 1)
    sig = jnp.where(s >= 0.0, 1.0, small) / (1.0 + small)
    grad = jnp.where(valid, sig - jnp.where(target, 1.0, 0.0), 0.0)
    grad_ref[...] = grad.astype(BF16)
    part = jnp.dot(own_columns(grad, per_dst), w_ref[...], preferred_element_type=F32)
    part = part.reshape(devs, sources, TILE, width)
    lane = iota((devs, TILE, LANES), 2)
    for i, (ret_ref, members) in enumerate(zip(ret_refs, outs)):
        before = carried if i == 0 else 0
        last = jnp.zeros((devs, TILE, LANES), F32)
        if before:
            end = before * per_source
            ret_ref[:, 0:end, :] = carry_ref[:, 0:end, :]
            last = carry_ref[:, end:, :].astype(F32)
        for j, source in enumerate(members):
            store_tiles(ret_ref, (before + j) * per_source, part[:, source])
            last = jnp.where(lane == before + j, loss[:, source], last)
        ret_ref[:, (before + len(members)) * per_source :, :] = last.astype(BF16)


def sources_of(x, width):
    return (x.shape[1] // TILE - 1) * LANES // width


def score(x, weights, count, block, outs, carry=None, params=PARAMS):
    devs, tile_rows, _ = x.shape
    per_dst = count.shape[0]
    all_labels, width = weights.shape
    labels = all_labels // per_dst
    slots = sources_of(x, width) * TILE
    carried = sources_of(carry, width) if carry is not None else 0
    sizes = [len(members) + (carried if i == 0 else 0) for i, members in enumerate(outs)]
    ret_rows = [(size * width // LANES + 1) * TILE for size in sizes]

    def by_dev(rows):
        return pl.BlockSpec((block, rows, LANES), lambda i: (i, 0, 0))

    return pl.pallas_call(
        functools.partial(score_kernel, per_dst=per_dst, carried=carried, outs=outs),
        grid=(devs // block,),
        out_shape=[jax.ShapeDtypeStruct((devs, r, LANES), BF16) for r in ret_rows]
        + [jax.ShapeDtypeStruct((devs * slots, labels), BF16)],
        in_specs=[
            pl.BlockSpec(memory_space=pltpu.SMEM),
            by_dev(tile_rows),
            whole((all_labels, width)),
        ]
        + ([by_dev(carry.shape[1])] if carried else []),
        out_specs=[by_dev(r) for r in ret_rows]
        + [pl.BlockSpec((block * slots, labels), lambda i: (i, 0))],
        compiler_params=params,
        cost_estimate=pl.CostEstimate(
            flops=4 * devs * slots * all_labels * width,
            bytes_accessed=4 * devs * slots * (width + labels) + 2 * all_labels * width,
            transcendentals=0,
        ),
        name="score",
    )(count, x, weights, *([carry] if carried else []))


def weight_kernel(*refs, per_dst):
    out_ref = refs[-1]
    width = out_ref.shape[1]
    total = None
    for x_ref, grad_ref in zip(refs[0:-1:2], refs[1:-1:2]):
        tiles, _ = load_tiles(x_ref[...], width)
        devs = x_ref.shape[0]
        x = jnp.concatenate([t.reshape(devs, 1, TILE, width) for t in tiles], axis=1)
        x = x.reshape(devs * len(tiles) * TILE, width).astype(BF16)
        grad = own_columns(grad_ref[...].astype(F32), per_dst)
        part = lax.dot_general(
            grad, x, (((0,), (0,)), ((), ())), preferred_element_type=F32
        )
        total = part if total is None else total + part

    @pl.when(pl.program_id(0) == 0)
    def _():
        out_ref[...] = total

    @pl.when(pl.program_id(0) > 0)
    def _():
        out_ref[...] += total


def weight_gradient(chunks, width, block, per_dst):
    labels = chunks[0][1].shape[1]
    all_labels = labels * per_dst
    devs = chunks[0][0].shape[0]
    rows = sum(grad.shape[0] for _, grad in chunks)
    flat = [a for chunk in chunks for a in chunk]
    specs = []
    for x, grad in chunks:
        specs.append(pl.BlockSpec((block,) + x.shape[1:], lambda i: (i, 0, 0)))
        specs.append(pl.BlockSpec((grad.shape[0] * block // devs, labels), lambda i: (i, 0)))
    return pl.pallas_call(
        functools.partial(weight_kernel, per_dst=per_dst),
        grid=(devs // block,),
        out_shape=jax.ShapeDtypeStruct((all_labels, width), F32),
        in_specs=specs,
        out_specs=whole((all_labels, width)),
        compiler_params=PARAMS,
        cost_estimate=pl.CostEstimate(
            flops=2 * rows * all_labels * width,
            bytes_accessed=2 * rows * (width + all_labels) + 4 * all_labels * width,
            transcendentals=0,
        ),
        name="weight_gradient",
    )(*flat)


def combine_kernel(ret_ref, *refs, order, picks, parts, added, width, steps):
    pick_refs, refs = refs[:picks], refs[picks:]
    add_refs, refs = dict(zip(added, refs[: len(added)])), refs[len(added) :]
    out_refs, ret = refs[: sum(parts)], refs[sum(parts)]
    held, sems = refs[sum(parts) + 1 : -1], refs[-1]
    dsts = ret_ref.shape[0] // steps
    queries = held[0].shape[2]
    rows = dsts * TILE
    over_rows = (((0,), (0,)), ((), ()))
    ats = [pl.ds(step * dsts, dsts) for step in range(steps)]
    pick_copies = [
        pltpu.make_async_copy(ref, place, sems.at[steps + i])
        for i, (ref, place) in enumerate(zip(pick_refs, held))
    ]
    ret_copies = [
        pltpu.make_async_copy(ret_ref.at[at], ret.at[at], sems.at[step]) for step, at in enumerate(ats)
    ]
    for copy in pick_copies + ret_copies:
        copy.start()
    for copy in pick_copies:
        copy.wait()
    totals = [None] * len(order)
    for step, at in enumerate(ats):
        ret_copies[step].wait()
        tiles, last = load_tiles(ret[at], width)
        for source, (which, index) in enumerate(order):
            pick = held[which][index, pl.ds(step * rows, rows), :]
            x = tiles[source].reshape(rows, width).astype(BF16)
            loss = jnp.dot(last, unit_row(source), preferred_element_type=F32).astype(BF16)
            x = jnp.concatenate([x, loss], axis=1)
            out = lax.dot_general(pick, x, over_rows, preferred_element_type=F32)
            totals[source] = out if step == 0 else totals[source] + out
    first = 0
    for source, count in enumerate(parts):
        out = totals[source]
        if source in add_refs:
            out = out + add_refs[source][...].astype(F32)
        part = queries // count
        for i in range(count):
            out_refs[first + i][...] = out[i * part : (i + 1) * part].astype(BF16)
        first += count


def combine(ret, picks, order, parts, width, arrived=(), params=SMALL):
    queries = picks[0].shape[2]
    shapes = [(queries // count, width + LANES) for count in parts for _ in range(count)]
    added = [a for _, a in arrived]
    steps = 1
    return pl.pallas_call(
        functools.partial(
            combine_kernel,
            order=order,
            picks=len(picks),
            parts=parts,
            added=[i for i, _ in arrived],
            width=width,
            steps=steps,
        ),
        out_shape=[jax.ShapeDtypeStruct(shape, BF16) for shape in shapes],
        in_specs=[IN_HBM] * (1 + len(picks)) + [IN_VMEM] * len(added),
        out_specs=[IN_VMEM] * len(shapes),
        scratch_shapes=[pltpu.VMEM(ret.shape, BF16)]
        + [pltpu.VMEM(pick.shape, BF16) for pick in picks]
        + [pltpu.SemaphoreType.DMA((steps + len(picks),))],
        compiler_params=params,
        name="combine",
    )(ret, *picks, *added)


def add(a, b):
    return (a.astype(F32) + b.astype(F32)).astype(BF16)


def add_half(a, half, second):
    zero = jnp.zeros_like(half)
    return add(a, jnp.concatenate([zero, half] if second else [half, zero], axis=0))


def finish_kernel(mine_ref, lower_ref, upper_ref, grad_ref, loss_ref, grad, loss, sems, *, scale):
    width = grad_ref.shape[1]
    total = mine_ref[...].astype(F32) + lower_ref[...].astype(F32) + upper_ref[...].astype(F32)
    grad[...] = total[:, 0:width].astype(BF16)
    grad_copy = pltpu.make_async_copy(grad, grad_ref, sems.at[0])
    grad_copy.start()
    loss[...] = total[:, width:].T[0:1] * scale
    loss_copy = pltpu.make_async_copy(loss, loss_ref, sems.at[1])
    loss_copy.start()
    grad_copy.wait()
    loss_copy.wait()


def finish(mine, to_lower, to_upper, scale):
    queries, wide = mine.shape
    width = wide - LANES
    return pl.pallas_call(
        functools.partial(finish_kernel, scale=scale),
        out_shape=(
            jax.ShapeDtypeStruct((queries, width), BF16),
            jax.ShapeDtypeStruct((1, queries), F32),
        ),
        in_specs=[IN_VMEM] * 3,
        out_specs=[IN_HBM] * 2,
        scratch_shapes=[
            pltpu.VMEM((queries, width), BF16),
            pltpu.VMEM((1, queries), F32),
            pltpu.SemaphoreType.DMA((2,)),
        ],
        compiler_params=SMALL,
        name="finish",
    )(mine, to_lower, to_upper)


def per_device(encodings, label_weights, label_count, matched, positive):
    queries, width = encodings.shape
    top = matched.shape[1]
    per_dst = label_count.shape[0]
    dsts = lax.axis_size("dev")
    groups = lax.axis_size("grp")
    labels = label_weights.shape[0] // per_dst
    half = queries // 2
    reach = groups // 2
    up_pairs = [(i, (i + 1) % groups) for i in range(groups)]
    down_pairs = [(i, (i - 1) % groups) for i in range(groups)]

    def up(v):
        return lax.ppermute(v, "grp", up_pairs)

    def down(v):
        return lax.ppermute(v, "grp", down_pairs)

    def exchange(v):
        return lax.all_to_all(v, "dev", split_axis=0, concat_axis=0, tiled=True)

    me = lax.axis_index("grp").astype(jnp.int32).reshape(1)
    own = prepare(encodings, matched, positive, per_dst * dsts)
    lower, upper = [own], [own]
    for _ in range(1, reach):
        lower.append(up(lower[-1]))
        upper.append(down(upper[-1]))
    across = (up(lower[-1][:half]), down(upper[-1][half:]))
    chunks = [
        [(own,)],
        [(v[k],) for k in range(1, reach - 1) for v in (lower, upper)],
        [(lower[-1],), (upper[-1],), across],
    ]
    picks, got = [], []
    for sources in chunks:
        send, pick = dispatch(sources, me, dsts, per_dst, top)
        if got:
            send, got[-1] = lax.optimization_barrier((send, got[-1]))
        got.append(exchange(send))
        picks.append(pick)

    block = min(16, dsts)
    mid = list(range(len(chunks[1])))
    part_own, grad_own = score(got[0], label_weights, label_count, block, [[0]], None, SMALL)
    part_near, part_mid, grad_mid = score(
        got[1], label_weights, label_count, block, [mid[:2], mid[2:]], part_own
    )
    part_mid, part_near = lax.optimization_barrier((part_mid, part_near))
    part_far, grad_far = score(got[2], label_weights, label_count, block, [[0, 1, 2]], part_mid)
    back_far = exchange(part_far)
    weight_grad = weight_gradient(list(zip(got, [grad_own, grad_mid, grad_far])), width, block, per_dst)
    part_near, back_far, weight_grad = lax.optimization_barrier((part_near, back_far, weight_grad))
    back_near = exchange(part_near)

    order = [(0, i) for i in mid[2:]] + [(1, 0), (1, 1), (1, 2)]
    parts = [1] * (len(order) - 1) + [2]
    sums = list(combine(back_far, picks[1:], order, parts, width, (), PARAMS))
    to_lower, to_upper = down(sums[-2]), up(sums[-1])
    sums = sums[:-2]
    sums[-2:] = [add_half(sums[-2], to_lower, False), add_half(sums[-1], to_upper, True)]
    to_lower, to_upper = down(sums[-2]), up(sums[-1])
    sums = sums[:-2]
    while sums:
        to_lower, to_upper = down(add(sums[-2], to_lower)), up(add(sums[-1], to_upper))
        sums = sums[:-2]
    order = [(0, 0), (1, 0), (1, 1)]
    arrived = ((1, to_lower), (2, to_upper))
    mine, a, b = combine(back_near, picks[:2], order, [1, 1, 1], width, arrived)
    to_lower, to_upper = down(a), up(b)
    enc_grad, query_loss = finish(mine, to_lower, to_upper, 1.0 / (top * labels))
    query_loss = query_loss.reshape(queries)
    return enc_grad, query_loss, weight_grad


def solution(mesh):
    in_specs = (
        P(("grp", "dev"), None),
        P(("grp", "dev"), None),
        P(("grp", "dev")),
        P(("grp", "dev"), None),
        P(("grp", "dev"), None),
    )
    out_specs = (P(("grp", "dev"), None), P(("grp", "dev")), P(("grp", "dev"), None))
    return jax.shard_map(
        per_device, mesh=mesh, in_specs=in_specs, out_specs=out_specs, check_vma=False
    )
```
